512 devices in a mesh: gx: 16 (over y_hi, x, core), gy: 32 (over z, y_lo).
Axes of the slice: x: 4, y: 4 (y_hi: 2, y_lo: 2; y = y_hi * 2 + y_lo), z: 16, core: 2. Of those that a mesh axis runs over, the one named last changes fastest.
Arguments:
- rel_pos: float32 [3, 10485760], P(None, ('gx', 'gy')), may hold values from -0.5 to 0.5
- charges: float32 [4, 10485760], P(None, ('gx', 'gy')), may hold values from -0.1875 to 0.1875
- block_cell: int32 [81920], P(('gx', 'gy')), may hold values from 0 to 127, as said below
- block_count: int32 [81920], P(('gx', 'gy')), may hold values from 1 to 128, as said below
- leaf_offsets: int32 [96, 3], replicated, may hold values from -3 to 3, as said below
- coarse_offsets: int32 [96, 3], replicated, may hold values from -3 to 3, as said below
- leaf_ops: float32 [96, 25, 25], replicated, may hold values from -0.125 to 0.125
- coarse_ops: float32 [96, 25, 25], replicated, may hold values from -0.125 to 0.125
- upward_ops: float32 [8, 25, 25], replicated, may hold values from -0.4375 to 0.4375
- downward_ops: float32 [8, 25, 25], replicated, may hold values from -1.25 to 1.25
Outputs:
- potential: float32 [4, 10485760], P(None, ('gx', 'gy'))
The draws below stay inside these ranges and needn't reach their ends.
Inputs may be any that keep to these rules, and one draw needn't show every extreme that they name: `block_cell`: within the 160 blocks of one column the values never fall, and every value 0 to 127 occurs. `block_count`: every block that is not the last block of its leaf cell holds 128 live atoms; the live atoms come first in a block. `leaf_offsets`: the rows are distinct offsets (dx, dy, dz) with |dx| <= 2, |dy| <= 2, |dz| <= 3 and max(|dx|, |dy|, |dz|) >= 2; (2, 0, 0), (-2, 0, 0), (0, 2, 0), (0, -2, 0), (0, 0, 3) and (0, 0, -3) are among them. `coarse_offsets`: the rows are distinct offsets (dx, dy, dz) with |dx| <= 2, |dy| <= 2, |dz| <= 3 and max(|dx|, |dy|, |dz|) >= 2; (2, 0, 0), (-2, 0, 0), (0, 2, 0), (0, -2, 0), (0, 0, 3) and (0, 0, -3) are among them.
All inputs are finite; a program needn't handle non-finite values.
Results may differ from the reference program's by a relative error of at most 0.0003.
Values sent between devices are 32-bit elements; how exact they have to be, the bound alone decides.
No kernel may reach another device: no remote copies, remote signals or barrier semaphores. Data moves between devices by JAX's collectives and lax.ppermute only.
A program may use at most 64 MiB of HBM per device.

```python
import math
import jax
import jax.numpy as jnp
import numpy as np
from jax import lax

Q = 4
P_SIZE = 25
NZ = 128
BLOCK = 128
BLK_DEV = 160
K1 = 96
K2 = 96
BLOCKS = 81920
ATOMS = 10485760
N_GX = 16
N_GY = 32


FORCED_ROWS = np.array([[2, 0, 0], [-2, 0, 0], [0, 2, 0], [0, -2, 0], [0, 0, 3], [0, 0, -3]], dtype=np.int32)


def candidate_table():
    rows_list = []
    for shift_x in range(-2, 3):
        for shift_y in range(-2, 3):
            for shift_z in range(-3, 4):
                reach_max = max(abs(shift_x), abs(shift_y), abs(shift_z))
                forced = abs(shift_x) == 2 and shift_y == 0 and (shift_z == 0) or (shift_x == 0 and abs(shift_y) == 2 and (shift_z == 0)) or (shift_x == 0 and shift_y == 0 and (abs(shift_z) == 3))
                if reach_max >= 2 and (not forced):
                    rows_list.append((shift_x, shift_y, shift_z))
    return np.array(rows_list, dtype=np.int32)


def offset_list(key, count):
    candidates = jnp.asarray(candidate_table())
    first_key, second_key = jax.random.split(key)
    picked = candidates[jax.random.permutation(first_key, candidates.shape[0])[:count - 6]]
    joined = jnp.concatenate([jnp.asarray(FORCED_ROWS), picked], axis=0)
    return joined[jax.random.permutation(second_key, count)].astype(jnp.int32)


def column_cells(key):
    columns = BLOCKS // BLK_DEV
    extra_cells = jax.random.randint(key, (columns, BLK_DEV - NZ), 0, NZ, dtype=jnp.int32)
    every_cell = jnp.broadcast_to(jnp.arange(NZ, dtype=jnp.int32)[None, :], (columns, NZ))
    return jnp.sort(jnp.concatenate([every_cell, extra_cells], axis=1), axis=1)


def draw_block_cell(key, part):
    cell_rows = column_cells(key)
    return cell_rows.reshape(-1).astype(jnp.int32)


def draw_block_count(key, part):
    cell_rows = column_cells(key)
    key = jax.random.fold_in(key, 7)
    changes = cell_rows[:, 1:] != cell_rows[:, :-1]
    last_block = jnp.concatenate([changes, jnp.ones((cell_rows.shape[0], 1), dtype=bool)], axis=1)
    partial_value = jax.random.randint(key, cell_rows.shape, 1, BLOCK + 1, dtype=jnp.int32)
    return jnp.where(last_block, partial_value, BLOCK).reshape(-1).astype(jnp.int32)


def draw_leaf_offsets(key, part):
    key = jax.random.fold_in(key, 3)
    return offset_list(key, K1)


def draw_coarse_offsets(key, part):
    key = jax.random.fold_in(key, 4)
    return offset_list(key, K2)


def steps_of(stream_key, extent, shards, least, high):
    def one(dim, blocks):
        heights = jax.random.uniform(jax.random.fold_in(jax.random.fold_in(stream_key, 6), dim), (blocks,), jnp.float32, least / len(shards), high / len(shards))
        return jnp.repeat(jnp.exp(heights), extent[dim] // blocks).reshape((-1,) + (1,) * (len(extent) - dim - 1))

    gain = one(*shards[0])
    for cut in shards[1:]:
        gain = gain * one(*cut)
    return gain


def normal_values(own_key, shape, deviation, limit, cuts=(), kind=jnp.bfloat16):
    entries = jax.random.normal(own_key, shape, jnp.float32) * deviation
    if len(cuts) > 0:
        entries = steps_of(own_key, shape, cuts, -0.22, 0.18) * entries
    return jnp.clip(entries, min=-limit, max=limit).astype(kind)


def setup_inputs(seed: int = 0) -> dict:
    seeds = jax.random.split(jax.random.key(seed), 11)
    rel_pos = jnp.clip(jax.random.uniform(seeds[0], (3, ATOMS), jnp.float32, -0.5, 0.5) * steps_of(seeds[0], (3, ATOMS), ((1, 512),), -0.4, 0.0), -0.5, 0.5)
    charges = normal_values(seeds[1], (Q, ATOMS), 0.03, 0.1875, ((1, 512),), jnp.float32)
    block_cell = draw_block_cell(jax.random.fold_in(seeds[10], 71), 0)
    block_count = draw_block_count(jax.random.fold_in(seeds[10], 71), 0)
    leaf_offsets = draw_leaf_offsets(jax.random.fold_in(seeds[10], 71), 0)
    coarse_offsets = draw_coarse_offsets(jax.random.fold_in(seeds[10], 71), 0)
    leaf_ops = normal_values(seeds[6], (K1, P_SIZE, P_SIZE), (P_SIZE * K1) ** -0.5, 0.125, (), jnp.float32)
    coarse_ops = normal_values(seeds[7], (K2, P_SIZE, P_SIZE), (P_SIZE * K2) ** -0.5, 0.125, (), jnp.float32)
    upward_ops = normal_values(seeds[8], (8, P_SIZE, P_SIZE), (8 * P_SIZE) ** -0.5, 0.4375, (), jnp.float32)
    downward_ops = normal_values(seeds[9], (8, P_SIZE, P_SIZE), P_SIZE ** -0.5, 1.25, (), jnp.float32)
    return dict(rel_pos=rel_pos, charges=charges, block_cell=block_cell, block_count=block_count, leaf_offsets=leaf_offsets, coarse_offsets=coarse_offsets, leaf_ops=leaf_ops, coarse_ops=coarse_ops, upward_ops=upward_ops, downward_ops=downward_ops)


PRECISE = lax.Precision.HIGHEST

def harmonics(rel_pos):
    point_x = 2.0 * rel_pos[0]
    point_y = 2.0 * rel_pos[1]
    point_z = 2.0 * rel_pos[2]
    radius_sq = point_x * point_x + point_y * point_y + point_z * point_z
    real_part = {(0, 0): jnp.ones_like(point_x)}
    imag_part = {(0, 0): jnp.zeros_like(point_x)}
    for degree in range(1, 5):
        lower_real = real_part[degree - 1, degree - 1]
        lower_imag = imag_part[degree - 1, degree - 1]
        real_part[degree, degree] = (point_x * lower_real - point_y * lower_imag) / (2.0 * degree)
        imag_part[degree, degree] = (point_x * lower_imag + point_y * lower_real) / (2.0 * degree)
        for azimuth in range(degree):
            scale_z = (2.0 * degree - 1.0) * point_z
            next_real = scale_z * real_part[degree - 1, azimuth]
            next_imag = scale_z * imag_part[degree - 1, azimuth]
            if degree - 2 >= azimuth:
                next_real = next_real - radius_sq * real_part[degree - 2, azimuth]
                next_imag = next_imag - radius_sq * imag_part[degree - 2, azimuth]
            divisor = float((degree + azimuth) * (degree - azimuth))
            real_part[degree, azimuth] = next_real / divisor
            imag_part[degree, azimuth] = next_imag / divisor
    rows_out = []
    for degree in range(5):
        rows_out.append(real_part[degree, 0] * float(math.factorial(degree)))
        for azimuth in range(1, degree + 1):
            factor = math.sqrt(math.factorial(degree + azimuth) * math.factorial(degree - azimuth))
            rows_out.append(real_part[degree, azimuth] * factor)
            rows_out.append(imag_part[degree, azimuth] * factor)
    return jnp.stack(rows_out)

def translate(moments, offsets, operators):

    def add_offset(running, column_entry):
        offset, operator = column_entry
        shifted = jnp.roll(moments, (-offset[0], -offset[1], -offset[2]), axis=(0, 1, 4))
        return (running + jnp.einsum('ji,xyqiz->xyqjz', operator, shifted, precision=PRECISE), None)
    running, unused = lax.scan(add_offset, jnp.zeros_like(moments), (offsets, operators))
    return running

def reference(rel_pos, charges, block_cell, block_count, leaf_offsets, coarse_offsets, leaf_ops, coarse_ops, upward_ops, downward_ops):
    columns = N_GX * N_GY
    per_column = BLK_DEV * BLOCK
    positions = rel_pos.reshape(3, columns, per_column).transpose(1, 0, 2)
    weights_q = charges.reshape(Q, columns, per_column).transpose(1, 0, 2)
    cell_rows = block_cell.reshape(columns, BLK_DEV)
    counts = block_count.reshape(columns, BLK_DEV)
    within = jnp.arange(BLOCK, dtype=jnp.int32)

    def live_of(count_row):
        return (within[None, :] < count_row[:, None]).astype(jnp.float32)

    def column_moments(column_entry):
        position, charge, cell_row, count_row = column_entry
        basis_rows = harmonics(position).reshape(P_SIZE, BLK_DEV, BLOCK)
        weighted = charge.reshape(Q, BLK_DEV, BLOCK) * live_of(count_row)[None]
        block_terms = jnp.einsum('qbt,jbt->bqj', weighted, basis_rows, precision=PRECISE)
        summed = jax.ops.segment_sum(block_terms, cell_row, num_segments=NZ)
        return summed.transpose(1, 2, 0)
    moments = lax.map(column_moments, (positions, weights_q, cell_rows, counts))
    moments = moments.reshape(N_GX, N_GY, Q, P_SIZE, NZ)
    leaf_local = translate(moments, leaf_offsets, leaf_ops)
    children = moments.reshape(N_GX // 2, 2, N_GY // 2, 2, Q, P_SIZE, NZ // 2, 2)
    coarse = jnp.einsum('XaYbqiZc,abcji->XYqjZ', children, upward_ops.reshape(2, 2, 2, P_SIZE, P_SIZE), precision=PRECISE)
    coarse_local = translate(coarse, coarse_offsets, coarse_ops)
    pushed = jnp.einsum('abcji,XYqiZ->XaYbqjZc', downward_ops.reshape(2, 2, 2, P_SIZE, P_SIZE), coarse_local, precision=PRECISE)
    local_total = leaf_local + pushed.reshape(N_GX, N_GY, Q, P_SIZE, NZ)
    local_total = local_total.reshape(columns, Q, P_SIZE, NZ)

    def column_potential(column_entry):
        position, cell_row, count_row, column_local = column_entry
        basis_rows = harmonics(position)
        atom_cell = jnp.repeat(cell_row, BLOCK)
        picked = jnp.take(column_local, atom_cell, axis=2)
        values = lax.optimization_barrier(jnp.sum(picked * basis_rows[None], axis=1))
        return values * live_of(count_row).reshape(-1)[None]
    potential = lax.map(column_potential, (positions, cell_rows, counts, local_total))
    return potential.transpose(1, 0, 2).reshape(Q, columns * per_column)
```

```python
import math

import jax
import jax.numpy as jnp
from jax import lax
from jax.experimental import pallas as pl
from jax.experimental.pallas import tpu as pltpu
from jax.sharding import PartitionSpec as P

NQ = 4
NP = 25
NZ = 128
BLKS = 160
LANES = 256
EXTRA = BLKS - 128
SLOT = 128
CLS = 96
PAD = 32
LEAF = 104
PAIR = 56
GROUP = 48
TILES = 13
DEPTH = TILES * NZ
F32 = jnp.float32
BF16 = jnp.bfloat16

VMEM = pl.BlockSpec(memory_space=pltpu.VMEM)
HBM = pl.BlockSpec(memory_space=pltpu.HBM)


def harmonics(pos_x, pos_y, pos_z):
    point_x = 2.0 * pos_x
    point_y = 2.0 * pos_y
    point_z = 2.0 * pos_z
    radius_sq = point_x * point_x + point_y * point_y + point_z * point_z
    real_part = {(0, 0): jnp.ones_like(point_x)}
    imag_part = {}
    for degree in range(1, 5):
        lower_real = real_part[degree - 1, degree - 1]
        if degree == 1:
            real_part[1, 1] = point_x * 0.5
            imag_part[1, 1] = point_y * 0.5
        else:
            lower_imag = imag_part[degree - 1, degree - 1]
            scale = 1.0 / (2.0 * degree)
            real_part[degree, degree] = (point_x * lower_real - point_y * lower_imag) * scale
            imag_part[degree, degree] = (point_x * lower_imag + point_y * lower_real) * scale
        for azimuth in range(degree):
            scale = 1.0 / float((degree + azimuth) * (degree - azimuth))
            scale_z = ((2.0 * degree - 1.0) * scale) * point_z
            if degree == 1:
                real_part[1, 0] = scale_z
                continue
            next_real = scale_z * real_part[degree - 1, azimuth]
            if degree - 2 >= azimuth:
                scaled_sq = radius_sq * scale
                next_real = next_real - scaled_sq * real_part[degree - 2, azimuth]
            real_part[degree, azimuth] = next_real
            if azimuth > 0:
                next_imag = scale_z * imag_part[degree - 1, azimuth]
                if degree - 2 >= azimuth:
                    next_imag = next_imag - scaled_sq * imag_part[degree - 2, azimuth]
                imag_part[degree, azimuth] = next_imag
    rows_out = []
    for degree in range(5):
        rows_out.append(real_part[degree, 0] * float(math.factorial(degree)))
        for azimuth in range(1, degree + 1):
            factor = math.sqrt(math.factorial(degree + azimuth) * math.factorial(degree - azimuth))
            rows_out.append(real_part[degree, azimuth] * factor)
            rows_out.append(imag_part[degree, azimuth] * factor)
    return rows_out


def split(value):
    high = value.astype(BF16)
    low = (value - high.astype(F32)).astype(BF16)
    return high, low


def dot(left, right):
    return lax.dot_general(left, right, (((1,), (0,)), ((), ())), preferred_element_type=F32)


def exact_dot(left, right):
    return lax.dot_general(
        left,
        right,
        (((1,), (0,)), ((), ())),
        preferred_element_type=F32,
        precision=lax.Precision.HIGHEST,
    )


def unpacked(field, channel, channels):
    zeros = jnp.zeros((PAD - NP, NZ), F32)
    return jnp.concatenate(
        [
            field[channel * 24 : channel * 24 + 24],
            field[channels * 24 + channel : channels * 24 + channel + 1],
            zeros,
        ],
        axis=0,
    )


def store_packed(ref, base, channel, channels, value):
    ref[base + channel * 24 : base + channel * 24 + 24, :] = value[:24]
    row = base + channels * 24 + channel
    ref[row : row + 1, :] = value[24:25]


def even_lanes(shape):
    return lax.broadcasted_iota(jnp.int32, shape, 1) % 2 == 0


def octant_rows(ref, octant):
    return ref.reshape(NP * 8, NP)[pl.ds(octant, NP, stride=8), :]


def parity(axis):
    return lax.rem(lax.axis_index(axis), 2)


def slots_down(tile):
    extra = tile[SLOT:, :]
    runs = [extra[:, g * EXTRA : (g + 1) * EXTRA] for g in range(4)]
    return jnp.concatenate([tile[:SLOT, :].T, jnp.concatenate(runs, axis=0).T], axis=0)


def blocks_down(tile):
    extra = tile[SLOT:, :].T
    runs = [extra[g * EXTRA : (g + 1) * EXTRA, :] for g in range(4)]
    return jnp.concatenate([tile[:SLOT, :].T, jnp.concatenate(runs, axis=1)], axis=0)


def spread_row(values, row):
    row[:, 0:SLOT] = values[:, 0:SLOT]
    for g in range(4):
        row[:, SLOT + g * EXTRA : SLOT + (g + 1) * EXTRA] = values[:, SLOT:BLKS]
    return row[...]


def member_t(cell_ref, row):
    cells = lax.broadcasted_iota(jnp.int32, (NZ, LANES), 0)
    return (cells == spread_row(cell_ref, row)).astype(F32)


def live_t(count_ref, row):
    counts = spread_row(count_ref, row)
    first = lax.broadcasted_iota(jnp.int32, (SLOT, SLOT), 0)
    run = lax.broadcasted_iota(jnp.int32, (EXTRA, SLOT), 1) // EXTRA
    second = lax.broadcasted_iota(jnp.int32, (EXTRA, SLOT), 0) + run * EXTRA
    return jnp.concatenate([first < counts[:, :SLOT], second < counts[:, SLOT:]], axis=0)


def moments_kernel(
    pos_in, charge_in, cell_in, count_in, upward_in, out, *scratch
):
    pos, charge, cell, count, upward, basis, weight, sums, row, ops, done = scratch
    copies = [
        pltpu.make_async_copy(source, target, done.at[n])
        for n, (source, target) in enumerate(
            (
                (pos_in, pos),
                (charge_in, charge),
                (cell_in, cell),
                (count_in, count),
                (upward_in, upward),
            )
        )
    ]
    for copy in copies:
        copy.start()
    copies[0].wait()
    coords = [slots_down(pos[:, d, :]) for d in range(3)]
    for j, value in enumerate(harmonics(*coords)):
        basis[j] = value
    for copy in copies[1:]:
        copy.wait()
    live = live_t(count, row)
    for q in range(NQ):
        weight[q] = jnp.where(live, slots_down(charge[:, q, :]), 0.0)
    sums[NQ * NP :, :] = jnp.zeros((LEAF - NQ * NP, LANES), F32)
    for j in range(NP):
        value = basis[j]
        for q in range(NQ):
            product = (weight[q] * value).reshape(BLKS // 8, 8, SLOT)
            at = q * 24 + j if j < 24 else 96 + q
            sums[at : at + 1, :SLOT] = jnp.sum(
                jnp.sum(product[: SLOT // 8], axis=0), axis=0, keepdims=True
            )
            sums[at : at + 1, SLOT:] = jnp.sum(
                jnp.sum(product[SLOT // 8 :], axis=0), axis=0, keepdims=True
            )
    member = member_t(cell, row).T.astype(BF16)
    high, low = split(sums[...])
    field = dot(high, member) + dot(low, member)
    out[0:LEAF, :] = field
    ops[...] = jnp.zeros_like(ops)
    octant = (parity("gx") * 2 + parity("gy")) * 2
    for c in range(2):
        ops[c * PAD : c * PAD + NP, 0:NP] = octant_rows(upward, octant + c)
    stacked = jnp.concatenate([unpacked(field, q, NQ) for q in range(NQ)], axis=1)
    raised = exact_dot(ops[...], stacked)
    out[LEAF : LEAF + PAIR, :] = jnp.zeros((PAIR, NZ), F32)
    even = even_lanes((PAD, NZ))
    for pair in range(2):
        first, second = [
            [raised[c * PAD : (c + 1) * PAD, q * NZ : (q + 1) * NZ] for c in range(2)]
            for q in (2 * pair, 2 * pair + 1)
        ]
        value = jnp.where(
            even,
            first[0] + pltpu.roll(first[1], NZ - 1, 1),
            pltpu.roll(second[0], 1, 1) + second[1],
        )
        store_packed(out, LEAF, pair, 2, value)


def tables_kernel(leaf_at, coarse_at, leaf_ops, coarse_ops, leaf_out, coarse_out, codes, left):
    toward = (1 - 2 * parity("gx")).astype(F32)
    lane = lax.broadcasted_iota(jnp.int32, (NZ, NZ), 1).astype(F32)
    for at, ops, out, columns in (
        (leaf_at, leaf_ops, leaf_out, 2),
        (coarse_at, coarse_ops, coarse_out, 1),
    ):
        codes[...] = jnp.full((8, NZ), 99.0, F32)
        codes[0:3, 0:CLS] = at[...].astype(F32)
        turned = codes[...].T
        place = (turned[:, 0:1] + 2.0) * 8.0 + 3.0 - turned[:, 2:3]
        ahead = -toward * turned[:, 1:2]
        picks = []
        for half in range(2):
            found = [lane == place + float(half * GROUP + t * 8) for t in range(columns)]
            picks.append(
                jnp.concatenate(
                    [
                        (found[t] & (ahead == float(r))).astype(F32)
                        for t in range(columns)
                        for r in range(3)
                    ],
                    axis=1,
                )
            )
        pick = jnp.concatenate(picks, axis=0).astype(BF16)
        left[...] = jnp.zeros_like(left)
        for i in range(NP):
            row = (i // 2) * PAD
            col = (i % 2) * NZ
            left[row : row + NP, col : col + CLS] = ops[:, i, :]
        blocks = 3 * columns
        for part, value in enumerate(split(left[...])):
            table = dot(value, pick).astype(BF16)
            for tile in range(TILES):
                for block in range(blocks):
                    row = (part * blocks + block) * PAD
                    out[row : row + PAD, tile * NZ : (tile + 1) * NZ] = table[
                        tile * PAD : (tile + 1) * PAD, block * NZ : (block + 1) * NZ
                    ]


def join_kernel(pairs, far, out):
    out[0:LEAF, :] = pairs[0, 0:LEAF, :]
    out[LEAF : 2 * LEAF, :] = pairs[1, 0:LEAF, :]
    out[2 * LEAF : 2 * LEAF + PAIR, :] = pairs[0, LEAF:, :] + pairs[1, LEAF:, :]
    out[2 * LEAF + PAIR :, :] = far[...]


def translate_kernel(near, sides, leaf_k, coarse_k, one_out, two_out, kept, *scratch):
    fields, high, low = scratch
    core = parity("gx")
    for ref in (high, low):
        for tile in range(TILES):
            used = 2 * GROUP if 2 * tile + 1 < NP else GROUP
            ref[tile * NZ + used : (tile + 1) * NZ, :] = jnp.zeros((NZ - used, NQ * NZ), BF16)

    def spread(columns, channels, step):
        for i in range(NP):
            row = (i // 2) * NZ + (i % 2) * GROUP
            for q in range(channels):
                at = q * 24 + i if i < 24 else channels * 24 + q
                for two in range(3):
                    turned = []
                    for column in columns[2 * two : 2 * two + 2]:
                        if column is None:
                            turned.append(jnp.zeros((8, NZ), F32))
                            continue
                        value = jnp.broadcast_to(fields[column, at : at + 1, :], (8, NZ))
                        turned.append(pltpu.roll(value, 0, 1, stride=step, stride_axis=0))
                    top, rest = split(jnp.concatenate(turned, axis=0))
                    base = row + two * 16
                    high[base : base + 16, q * NZ : (q + 1) * NZ] = top
                    low[base : base + 16, q * NZ : (q + 1) * NZ] = rest

    def product(table, height, width):
        both = dot(table[...], high[:, :width])
        return both[:height] + both[height:] + dot(table[0:height, :], low[:, :width])

    def emit(ref, base, value, channels, rows):
        ref[base + channels * 25 : base + rows, :] = jnp.zeros((rows - channels * 25, NZ), F32)
        for q in range(channels):
            store_packed(ref, base, q, channels, value[:, q * NZ : (q + 1) * NZ])

    def back(value, step):
        return pltpu.roll(value, NZ - 3 * step, 1)

    for a in range(2):
        fields[a] = back(sides[0, a * LEAF : (a + 1) * LEAF, :], 1)
        fields[2 + a] = back(near[a, 0:LEAF, :], 1)
        fields[4 + a] = back(sides[1, a * LEAF : (a + 1) * LEAF, :], 1)
    spread(range(6), NQ, 1)
    result = product(leaf_k, 6 * PAD, NQ * NZ)
    blocks = [result[b * PAD : (b + 1) * PAD] for b in range(6)]
    for t in range(2):
        emit(one_out, t * LEAF, blocks[3 * t + 1], NQ, LEAF)
        emit(two_out, t * LEAF, blocks[3 * t + 2], NQ, LEAF)
    emit(kept, 0, jnp.where(core == 0, blocks[0], blocks[3]), NQ, LEAF)

    one, two = 2 * LEAF, 2 * LEAF + PAIR
    fields[0, 0:PAIR, :] = back(sides[0, two:, :], 2)
    fields[1, 0:PAIR, :] = back(sides[0, one:two, :], 2)
    fields[2, 0:PAIR, :] = back(near[0, LEAF:, :] + near[1, LEAF:, :], 2)
    fields[3, 0:PAIR, :] = back(sides[1, one:two, :], 2)
    fields[4, 0:PAIR, :] = back(sides[1, two:, :], 2)
    spread([0, 1, 2, 3, 4, None], 2, 2)
    result = product(coarse_k, 3 * PAD, 2 * NZ)
    blocks = [result[b * PAD : (b + 1) * PAD] for b in range(3)]
    outer = lax.rem(core + parity("gy"), 2) == 1
    emit(kept, LEAF, jnp.where(core == 0, blocks[0], 0.0), 2, PAIR)
    emit(kept, LEAF + PAIR, jnp.where(outer, blocks[2], blocks[1]), 2, PAIR)
    emit(one_out, 2 * LEAF, jnp.where(outer, blocks[1], blocks[0]), 2, PAIR)
    emit(one_out, 2 * LEAF + PAIR, blocks[2], 2, PAIR)
    emit(two_out, 2 * LEAF, blocks[1], 2, PAIR)
    emit(two_out, 2 * LEAF + PAIR, jnp.where(outer, 0.0, blocks[2]), 2, PAIR)


def relay_kernel(kept, one_in, two_in, out):
    relayed = one_in[2 * LEAF + PAIR :, :] + two_in[2 * LEAF + PAIR :, :]
    out[...] = kept[LEAF + PAIR :, :] + relayed


def exchange_kernel(kept, one_in, two_in, three_in, out):
    there = pl.ds(pl.multiple_of((1 - parity("gx")) * LEAF, 8), LEAF)
    out[0:LEAF, :] = one_in[there, :] + two_in[there, :]
    direct = pl.ds(2 * LEAF, PAIR)
    out[LEAF:, :] = kept[LEAF : LEAF + PAIR, :] + (
        one_in[direct, :] + two_in[direct, :] + three_in[...]
    )


def basis_kernel(pos, after, basis):
    del after
    coords = [slots_down(pos[:, d, :]) for d in range(3)]
    for j, value in enumerate(harmonics(*coords)):
        basis[j] = value


def potential_kernel(
    kept, one_in, two_in, last, cell, count, downward, basis, out, row, ops, spread, result
):
    core = parity("gx")
    mine = pl.ds(pl.multiple_of(core * LEAF, 8), LEAF)
    leaf = kept[0:LEAF, :] + one_in[mine, :] + two_in[mine, :] + last[1 - core, 0:LEAF, :]
    coarse = last[0, LEAF:, :] + last[1, LEAF:, :]
    ops[...] = jnp.zeros_like(ops)
    octant = (parity("gx") * 2 + parity("gy")) * 2
    for c in range(2):
        ops[0:NP, c * PAD : c * PAD + NP] = octant_rows(downward, octant + c)
    even = even_lanes((PAD, NZ))
    columns = []
    for q in range(NQ):
        value = unpacked(coarse, q // 2, 2)
        if q % 2 == 0:
            down = [jnp.where(even, value, 0.0), jnp.where(even, 0.0, pltpu.roll(value, 1, 1))]
        else:
            down = [jnp.where(even, pltpu.roll(value, NZ - 1, 1), 0.0), jnp.where(even, 0.0, value)]
        columns.append(jnp.concatenate(down, axis=0))
    pushed = exact_dot(ops[0:PAD, :], jnp.concatenate(columns, axis=1))
    local = jnp.concatenate(
        [unpacked(leaf, q, NQ) + pushed[:, q * NZ : (q + 1) * NZ] for q in range(NQ)], axis=0
    )
    member = member_t(cell, row).astype(BF16)
    high, low = split(local)
    spread[...] = dot(high, member) + dot(low, member)
    live = live_t(count, row)
    for start, size, lane in ((0, 64, 0), (64, 64, 0), (SLOT, EXTRA, SLOT)):
        totals = [None] * NQ
        for j in range(NP):
            value = basis[j, start : start + size, :]
            for q in range(NQ):
                term = spread[q * PAD + j : q * PAD + j + 1, lane : lane + SLOT] * value
                totals[q] = term if j == 0 else totals[q] + term
        for q in range(NQ):
            result[q, start : start + size, :] = totals[q]
    for q in range(NQ):
        out[:, q, :] = blocks_down(jnp.where(live, result[q], 0.0))


def call(kernel, outs, scratch, specs, name, micros=1, megabytes=24.0):
    return pl.pallas_call(
        kernel,
        out_shape=outs if len(outs) > 1 else outs[0],
        in_specs=specs,
        out_specs=[VMEM] * len(outs) if len(outs) > 1 else VMEM,
        scratch_shapes=scratch,
        cost_estimate=pl.CostEstimate(
            flops=int(micros * 1e9), bytes_accessed=1000000, transcendentals=0
        ),
        compiler_params=pltpu.CompilerParams(vmem_limit_bytes=int(megabytes * 1024 * 1024)),
        name=name,
    )


def rows(count):
    return jax.ShapeDtypeStruct((count, NZ), F32)


def chip_pairs():
    return [[i, i + 1] for i in range(0, lax.axis_size("gx"), 2)]


def outward_x(distance):
    peers = lax.axis_size("gx")
    return [(i, (i + distance if i % 2 else i - distance) % peers) for i in range(peers)]


def along_y(field, distance):
    wide, tall = lax.axis_size("gx"), lax.axis_size("gy")
    route = []
    for x in range(wide):
        step = -distance if x % 2 else distance
        route += [(x * tall + y, x * tall + (y + step) % tall) for y in range(tall)]
    return lax.ppermute(field, ("gx", "gy"), route)


def per_device(
    rel_pos,
    charges,
    block_cell,
    block_count,
    leaf_offsets,
    coarse_offsets,
    leaf_ops,
    coarse_ops,
    upward_ops,
    downward_ops,
):
    pos = rel_pos.reshape(3, BLKS, SLOT).transpose(1, 0, 2)
    charge = charges.reshape(NQ, BLKS, SLOT).transpose(1, 0, 2)
    cell = block_cell.reshape(1, BLKS)
    count = block_count.reshape(1, BLKS)
    upward = upward_ops.transpose(1, 0, 2)
    downward = downward_ops.transpose(1, 0, 2)
    index_row = pltpu.VMEM((1, LANES), jnp.int32)

    own_field = call(
        moments_kernel,
        [rows(LEAF + PAIR)],
        [
            pltpu.VMEM((BLKS, 3, SLOT), F32),
            pltpu.VMEM((BLKS, NQ, SLOT), F32),
            pltpu.VMEM((1, BLKS), jnp.int32),
            pltpu.VMEM((1, BLKS), jnp.int32),
            pltpu.VMEM((NP, 8, NP), F32),
            pltpu.VMEM((NP, BLKS, SLOT), F32),
            pltpu.VMEM((NQ, BLKS, SLOT), F32),
            pltpu.VMEM((LEAF, LANES), F32),
            index_row,
            pltpu.VMEM((2 * PAD, PAD), F32),
            pltpu.SemaphoreType.DMA((5,)),
        ],
        [HBM] * 5,
        "moments",
        3,
        63.9,
    )(pos, charge, cell, count, upward)

    near = lax.all_gather(own_field, "gx", axis_index_groups=chip_pairs())
    beside = lax.ppermute(near, "gx", outward_x(1))
    parents = near[0, LEAF:] + near[1, LEAF:]
    beyond = lax.ppermute(parents, "gx", outward_x(3))
    leaf_k, coarse_k = call(
        tables_kernel,
        [
            jax.ShapeDtypeStruct((12 * PAD, DEPTH), BF16),
            jax.ShapeDtypeStruct((6 * PAD, DEPTH), BF16),
        ],
        [pltpu.VMEM((8, NZ), F32), pltpu.VMEM((TILES * PAD, 2 * NZ), F32)],
        [VMEM] * 4,
        "tables",
        2,
    )(
        leaf_offsets.T,
        coarse_offsets.T,
        leaf_ops.transpose(1, 2, 0),
        coarse_ops.transpose(1, 2, 0),
    )
    side = call(join_kernel, [rows(2 * LEAF + 2 * PAIR)], [], [VMEM] * 2, "join")(beside, beyond)
    sides = lax.all_gather(side, "gx", axis_index_groups=chip_pairs())

    one, two, kept = call(
        translate_kernel,
        [rows(2 * LEAF + 2 * PAIR), rows(2 * LEAF + 2 * PAIR), rows(LEAF + 2 * PAIR)],
        [pltpu.VMEM((6, LEAF, NZ), F32)] + [pltpu.VMEM((DEPTH, NQ * NZ), BF16)] * 2,
        [VMEM] * 4,
        "translate",
        3,
    )(near, sides, leaf_k, coarse_k)

    one = along_y(one, 1)
    two = along_y(two, 2)
    relayed = call(relay_kernel, [rows(PAIR)], [], [VMEM] * 3, "relay")(kept, one, two)
    three = along_y(relayed, 3)
    basis = call(
        basis_kernel,
        [jax.ShapeDtypeStruct((NP, BLKS, SLOT), F32)],
        [],
        [VMEM] * 2,
        "basis",
    )(pos, kept)
    passed = call(exchange_kernel, [rows(LEAF + PAIR)], [], [VMEM] * 4, "exchange")(
        kept, one, two, three
    )
    last = lax.all_gather(passed, "gx", axis_index_groups=chip_pairs())

    potential = call(
        potential_kernel,
        [jax.ShapeDtypeStruct((BLKS, NQ, SLOT), F32)],
        [
            index_row,
            pltpu.VMEM((PAD, 2 * PAD), F32),
            pltpu.VMEM((NQ * PAD, LANES), F32),
            pltpu.VMEM((NQ, BLKS, SLOT), F32),
        ],
        [VMEM] * 8,
        "potential",
        3,
    )(kept, one, two, last, cell, count, downward, basis)
    return potential.transpose(1, 0, 2).reshape(NQ, BLKS * SLOT)


def solution(mesh):
    in_specs = (
        P(None, ("gx", "gy")),
        P(None, ("gx", "gy")),
        P(("gx", "gy")),
        P(("gx", "gy")),
        P(),
        P(),
        P(),
        P(),
        P(),
        P(),
    )
    out_specs = P(None, ("gx", "gy"))
    return jax.shard_map(
        per_device, mesh=mesh, in_specs=in_specs, out_specs=out_specs, check_vma=False
    )
```

```python
import math

import jax
import jax.numpy as jnp
from jax import lax
from jax.experimental import pallas as pl
from jax.experimental.pallas import tpu as pltpu
from jax.sharding import PartitionSpec as P

NQ = 4
NP = 25
NZ = 128
BLKS = 160
LANES = 256
EXTRA = BLKS - 128
SLOT = 128
CLS = 96
PAD = 32
LEAF = 104
PAIR = 56
GROUP = 48
TILES = 13
DEPTH = TILES * NZ
F32 = jnp.float32
BF16 = jnp.bfloat16

VMEM = pl.BlockSpec(memory_space=pltpu.VMEM)
HBM = pl.BlockSpec(memory_space=pltpu.HBM)


def harmonics(pos_x, pos_y, pos_z):
    point_x = 2.0 * pos_x
    point_y = 2.0 * pos_y
    point_z = 2.0 * pos_z
    radius_sq = point_x * point_x + point_y * point_y + point_z * point_z
    real_part = {(0, 0): jnp.ones_like(point_x)}
    imag_part = {}
    for degree in range(1, 5):
        lower_real = real_part[degree - 1, degree - 1]
        if degree == 1:
            real_part[1, 1] = point_x * 0.5
            imag_part[1, 1] = point_y * 0.5
        else:
            lower_imag = imag_part[degree - 1, degree - 1]
            scale = 1.0 / (2.0 * degree)
            real_part[degree, degree] = (point_x * lower_real - point_y * lower_imag) * scale
            imag_part[degree, degree] = (point_x * lower_imag + point_y * lower_real) * scale
        for azimuth in range(degree):
            scale = 1.0 / float((degree + azimuth) * (degree - azimuth))
            scale_z = ((2.0 * degree - 1.0) * scale) * point_z
            if degree == 1:
                real_part[1, 0] = scale_z
                continue
            next_real = scale_z * real_part[degree - 1, azimuth]
            if degree - 2 >= azimuth:
                scaled_sq = radius_sq * scale
                next_real = next_real - scaled_sq * real_part[degree - 2, azimuth]
            real_part[degree, azimuth] = next_real
            if azimuth > 0:
                next_imag = scale_z * imag_part[degree - 1, azimuth]
                if degree - 2 >= azimuth:
                    next_imag = next_imag - scaled_sq * imag_part[degree - 2, azimuth]
                imag_part[degree, azimuth] = next_imag
    rows_out = []
    for degree in range(5):
        rows_out.append(real_part[degree, 0] * float(math.factorial(degree)))
        for azimuth in range(1, degree + 1):
            factor = math.sqrt(math.factorial(degree + azimuth) * math.factorial(degree - azimuth))
            rows_out.append(real_part[degree, azimuth] * factor)
            rows_out.append(imag_part[degree, azimuth] * factor)
    return rows_out


def split(value):
    high = value.astype(BF16)
    low = (value - high.astype(F32)).astype(BF16)
    return high, low


def dot(left, right):
    return lax.dot_general(left, right, (((1,), (0,)), ((), ())), preferred_element_type=F32)


def exact_dot(left, right):
    high, low = split(left)
    top, rest = split(right)
    both = dot(jnp.concatenate([high, low], axis=0), top)
    return both[: left.shape[0]] + both[left.shape[0] :] + dot(high, rest)


def unpacked(field, channel, channels):
    zeros = jnp.zeros((PAD - NP, NZ), F32)
    return jnp.concatenate(
        [
            field[channel * 24 : channel * 24 + 24],
            field[channels * 24 + channel : channels * 24 + channel + 1],
            zeros,
        ],
        axis=0,
    )


def store_packed(ref, base, channel, channels, value):
    ref[base + channel * 24 : base + channel * 24 + 24, :] = value[:24]
    row = base + channels * 24 + channel
    ref[row : row + 1, :] = value[24:25]


def even_lanes(shape):
    return lax.broadcasted_iota(jnp.int32, shape, 1) % 2 == 0


def octant_rows(ref, octant):
    return ref.reshape(NP * 8, NP)[pl.ds(octant, NP, stride=8), :]


def parity(axis):
    return lax.rem(lax.axis_index(axis), 2)


def slots_down(tile):
    extra = tile[SLOT:, :]
    runs = [extra[:, g * EXTRA : (g + 1) * EXTRA] for g in range(4)]
    return jnp.concatenate([tile[:SLOT, :].T, jnp.concatenate(runs, axis=0).T], axis=0)


def blocks_down(tile):
    extra = tile[SLOT:, :].T
    runs = [extra[g * EXTRA : (g + 1) * EXTRA, :] for g in range(4)]
    return jnp.concatenate([tile[:SLOT, :].T, jnp.concatenate(runs, axis=1)], axis=0)


def spread_row(values, row):
    row[:, 0:SLOT] = values[:, 0:SLOT]
    for g in range(4):
        row[:, SLOT + g * EXTRA : SLOT + (g + 1) * EXTRA] = values[:, SLOT:BLKS]
    return row[...]


def member_t(cell_ref, row):
    cells = lax.broadcasted_iota(jnp.int32, (NZ, LANES), 0)
    return (cells == spread_row(cell_ref, row)).astype(F32)


def live_t(count_ref, row):
    counts = spread_row(count_ref, row)
    first = lax.broadcasted_iota(jnp.int32, (SLOT, SLOT), 0)
    run = lax.broadcasted_iota(jnp.int32, (EXTRA, SLOT), 1) // EXTRA
    second = lax.broadcasted_iota(jnp.int32, (EXTRA, SLOT), 0) + run * EXTRA
    return jnp.concatenate([first < counts[:, :SLOT], second < counts[:, SLOT:]], axis=0)


def moments_kernel(
    pos_in, charge_in, cell_in, count_in, upward_in, out, *scratch
):
    pos, charge, cell, count, upward, basis, weight, sums, row, ops, done = scratch
    copies = [
        pltpu.make_async_copy(source, target, done.at[n])
        for n, (source, target) in enumerate(
            (
                (pos_in, pos),
                (charge_in, charge),
                (cell_in, cell),
                (count_in, count),
                (upward_in, upward),
            )
        )
    ]
    for copy in copies:
        copy.start()
    copies[0].wait()
    coords = [slots_down(pos[:, d, :]) for d in range(3)]
    for j, value in enumerate(harmonics(*coords)):
        basis[j] = value
    for copy in copies[1:]:
        copy.wait()
    live = live_t(count, row)
    for q in range(NQ):
        weight[q] = jnp.where(live, slots_down(charge[:, q, :]), 0.0)
    sums[NQ * NP :, :] = jnp.zeros((LEAF - NQ * NP, LANES), F32)
    for j in range(NP):
        value = basis[j]
        for q in range(NQ):
            product = (weight[q] * value).reshape(BLKS // 8, 8, SLOT)
            at = q * 24 + j if j < 24 else 96 + q
            sums[at : at + 1, :SLOT] = jnp.sum(
                jnp.sum(product[: SLOT // 8], axis=0), axis=0, keepdims=True
            )
            sums[at : at + 1, SLOT:] = jnp.sum(
                jnp.sum(product[SLOT // 8 :], axis=0), axis=0, keepdims=True
            )
    member = member_t(cell, row).T.astype(BF16)
    high, low = split(sums[...])
    field = dot(high, member) + dot(low, member)
    out[0:LEAF, :] = field
    ops[...] = jnp.zeros_like(ops)
    octant = (parity("gx") * 2 + parity("gy")) * 2
    for c in range(2):
        ops[c * PAD : c * PAD + NP, 0:NP] = octant_rows(upward, octant + c)
    stacked = jnp.concatenate([unpacked(field, q, NQ) for q in range(NQ)], axis=1)
    raised = exact_dot(ops[...], stacked)
    out[LEAF : LEAF + PAIR, :] = jnp.zeros((PAIR, NZ), F32)
    even = even_lanes((PAD, NZ))
    for pair in range(2):
        first, second = [
            [raised[c * PAD : (c + 1) * PAD, q * NZ : (q + 1) * NZ] for c in range(2)]
            for q in (2 * pair, 2 * pair + 1)
        ]
        value = jnp.where(
            even,
            first[0] + pltpu.roll(first[1], NZ - 1, 1),
            pltpu.roll(second[0], 1, 1) + second[1],
        )
        store_packed(out, LEAF, pair, 2, value)


def tables_kernel(leaf_at, coarse_at, leaf_ops, coarse_ops, leaf_out, coarse_out, codes, left):
    toward = (1 - 2 * parity("gx")).astype(F32)
    lane = lax.broadcasted_iota(jnp.int32, (NZ, NZ), 1).astype(F32)
    for at, ops, out, columns in (
        (leaf_at, leaf_ops, leaf_out, 2),
        (coarse_at, coarse_ops, coarse_out, 1),
    ):
        reaches = (0, 1, 2) if columns == 2 else (0, 1, 2, -1, -2)
        codes[...] = jnp.full((8, NZ), 99.0, F32)
        codes[0:3, 0:CLS] = at[...].astype(F32)
        turned = codes[...].T
        place = (turned[:, 0:1] + 2.0) * 8.0 + 3.0 - turned[:, 2:3]
        ahead = -toward * turned[:, 1:2]
        picks = []
        for half in range(2):
            found = [lane == place + float(half * GROUP + t * 8) for t in range(columns)]
            picks.append(
                jnp.concatenate(
                    [
                        (found[t] & (ahead == float(r))).astype(F32)
                        for t in range(columns)
                        for r in reaches
                    ],
                    axis=1,
                )
            )
        pick = jnp.concatenate(picks, axis=0).astype(BF16)
        left[...] = jnp.zeros_like(left)
        for i in range(NP):
            row = (i // 2) * PAD
            col = (i % 2) * NZ
            left[row : row + NP, col : col + CLS] = ops[:, i, :]
        blocks = columns * len(reaches)
        for part, value in enumerate(split(left[...])):
            table = dot(value, pick).astype(BF16)
            for tile in range(TILES):
                for block in range(blocks):
                    row = (part * blocks + block) * PAD
                    out[row : row + PAD, tile * NZ : (tile + 1) * NZ] = table[
                        tile * PAD : (tile + 1) * PAD, block * NZ : (block + 1) * NZ
                    ]


def pair_kernel(near, fields, parents):
    fields[0:LEAF, :] = near[0, 0:LEAF, :]
    fields[LEAF : 2 * LEAF, :] = near[1, 0:LEAF, :]
    total = near[0, LEAF:, :] + near[1, LEAF:, :]
    fields[2 * LEAF :, :] = total
    parents[...] = total


def join_kernel(fields, far, out):
    out[0 : 2 * LEAF + PAIR, :] = fields[...]
    out[2 * LEAF + PAIR :, :] = far[...]


def translate_kernel(near, sides, leaf_k, coarse_k, one_out, two_out, kept, *scratch):
    fields, parents, high, low, coarse_high, coarse_low = scratch
    core = parity("gx")
    for ref in (high, low, coarse_high, coarse_low):
        for tile in range(TILES):
            used = 2 * GROUP if 2 * tile + 1 < NP else GROUP
            ref[tile * NZ + used : (tile + 1) * NZ, :] = jnp.zeros(
                (NZ - used, ref.shape[1]), BF16
            )

    def spread(source, columns, high, low, step):
        channels = high.shape[1] // NZ

        def turned(part, column, at):
            if column is None:
                return jnp.zeros((8, NZ), F32)
            value = jnp.broadcast_to(source[part, column, at : at + 1, :], (8, NZ))
            return pltpu.roll(value, 0, 1, stride=step, stride_axis=0)

        for i in range(NP):
            row = (i // 2) * NZ + (i % 2) * GROUP
            for q in range(channels):
                at = q * 24 + i if i < 24 else channels * 24 + q
                for two in range(3):
                    base = row + two * 16
                    for part, ref in enumerate((high, low)):
                        value = jnp.concatenate(
                            [turned(part, column, at) for column in columns[2 * two : 2 * two + 2]],
                            axis=0,
                        )
                        ref[base : base + 16, q * NZ : (q + 1) * NZ] = value.astype(BF16)

    def product(table, height, high, low):
        both = dot(table[...], high[...])
        return both[:height] + both[height:] + dot(table[0:height, :], low[...])

    def emit(ref, base, value, channels, rows):
        ref[base + channels * 25 : base + rows, :] = jnp.zeros((rows - channels * 25, NZ), F32)
        for q in range(channels):
            store_packed(ref, base, q, channels, value[:, q * NZ : (q + 1) * NZ])

    def back(target, column, value, step):
        value = pltpu.roll(value, NZ - 3 * step, 1)
        top = value.astype(BF16).astype(F32)
        target[0, column] = top
        target[1, column] = value - top

    one, two = 2 * LEAF, 2 * LEAF + PAIR
    back(parents, 0, sides[0, two:, :], 2)
    back(parents, 1, sides[0, one:two, :], 2)
    back(parents, 2, near[one:, :], 2)
    back(parents, 3, sides[1, one:two, :], 2)
    back(parents, 4, sides[1, two:, :], 2)
    for a in range(2):
        back(fields, a, sides[0, a * LEAF : (a + 1) * LEAF, :], 1)
        back(fields, 2 + a, near[a * LEAF : (a + 1) * LEAF, :], 1)
        back(fields, 4 + a, sides[1, a * LEAF : (a + 1) * LEAF, :], 1)
    spread(parents, [0, 1, 2, 3, 4, None], coarse_high, coarse_low, 2)
    spread(fields, range(6), high, low, 1)
    result = product(coarse_k, 5 * PAD, coarse_high, coarse_low)
    coarse = [result[b * PAD : (b + 1) * PAD] for b in range(5)]
    result = product(leaf_k, 6 * PAD, high, low)
    blocks = [result[b * PAD : (b + 1) * PAD] for b in range(6)]
    for t in range(2):
        emit(one_out, t * LEAF, blocks[3 * t + 1], NQ, LEAF)
        emit(two_out, t * LEAF, blocks[3 * t + 2], NQ, LEAF)
    emit(kept, 0, jnp.where(core == 0, blocks[0], blocks[3]), NQ, LEAF)
    blocks = coarse
    outer = lax.rem(core + parity("gy"), 2) == 1
    emit(kept, LEAF, jnp.where(core == 0, blocks[0], 0.0), 2, PAIR)
    emit(kept, LEAF + PAIR, jnp.where(outer, blocks[3], blocks[4]), 2, PAIR)
    emit(one_out, 2 * LEAF, jnp.where(outer, blocks[1], blocks[0]), 2, PAIR)
    emit(one_out, 2 * LEAF + PAIR, blocks[2], 2, PAIR)
    emit(two_out, 2 * LEAF, blocks[1], 2, PAIR)
    emit(two_out, 2 * LEAF + PAIR, jnp.where(outer, 0.0, blocks[2]), 2, PAIR)


def relay_kernel(kept, one_in, two_in, out):
    relayed = one_in[2 * LEAF + PAIR :, :] + two_in[2 * LEAF + PAIR :, :]
    out[...] = kept[LEAF + PAIR :, :] + relayed


def exchange_kernel(kept, one_in, two_in, three_in, out):
    there = pl.ds(pl.multiple_of((1 - parity("gx")) * LEAF, 8), LEAF)
    out[0:LEAF, :] = one_in[there, :] + two_in[there, :]
    direct = pl.ds(2 * LEAF, PAIR)
    out[LEAF:, :] = kept[LEAF : LEAF + PAIR, :] + (
        one_in[direct, :] + two_in[direct, :] + three_in[parity("gx")]
    )


def basis_kernel(pos, after, basis):
    del after
    coords = [slots_down(pos[:, d, :]) for d in range(3)]
    for j, value in enumerate(harmonics(*coords)):
        basis[j] = value


def potential_kernel(
    kept, one_in, two_in, last, cell, count, downward, basis, out, row, ops, spread, result
):
    core = parity("gx")
    mine = pl.ds(pl.multiple_of(core * LEAF, 8), LEAF)
    leaf = kept[0:LEAF, :] + one_in[mine, :] + two_in[mine, :] + last[1 - core, 0:LEAF, :]
    coarse = last[0, LEAF:, :] + last[1, LEAF:, :]
    ops[...] = jnp.zeros_like(ops)
    octant = (parity("gx") * 2 + parity("gy")) * 2
    for c in range(2):
        ops[0:NP, c * PAD : c * PAD + NP] = octant_rows(downward, octant + c)
    even = even_lanes((PAD, NZ))
    columns = []
    for q in range(NQ):
        value = unpacked(coarse, q // 2, 2)
        if q % 2 == 0:
            down = [jnp.where(even, value, 0.0), jnp.where(even, 0.0, pltpu.roll(value, 1, 1))]
        else:
            down = [jnp.where(even, pltpu.roll(value, NZ - 1, 1), 0.0), jnp.where(even, 0.0, value)]
        columns.append(jnp.concatenate(down, axis=0))
    pushed = exact_dot(ops[0:PAD, :], jnp.concatenate(columns, axis=1))
    local = jnp.concatenate(
        [unpacked(leaf, q, NQ) + pushed[:, q * NZ : (q + 1) * NZ] for q in range(NQ)], axis=0
    )
    member = member_t(cell, row).astype(BF16)
    high, low = split(local)
    spread[...] = dot(high, member) + dot(low, member)
    live = live_t(count, row)
    for start, size, lane in ((0, 64, 0), (64, 64, 0), (SLOT, EXTRA, SLOT)):
        totals = [None] * NQ
        for j in range(NP):
            value = basis[j, start : start + size, :]
            for q in range(NQ):
                term = spread[q * PAD + j : q * PAD + j + 1, lane : lane + SLOT] * value
                totals[q] = term if j == 0 else totals[q] + term
        for q in range(NQ):
            result[q, start : start + size, :] = totals[q]
    for q in range(NQ):
        out[:, q, :] = blocks_down(jnp.where(live, result[q], 0.0))


def call(kernel, outs, scratch, specs, name, micros=1):
    return pl.pallas_call(
        kernel,
        out_shape=outs if len(outs) > 1 else outs[0],
        in_specs=specs,
        out_specs=[VMEM] * len(outs) if len(outs) > 1 else VMEM,
        scratch_shapes=scratch,
        cost_estimate=pl.CostEstimate(
            flops=int(micros * 1e9), bytes_accessed=1000000, transcendentals=0
        ),
        compiler_params=pltpu.CompilerParams(vmem_limit_bytes=24 * 1024 * 1024),
        name=name,
    )


def rows(count):
    return jax.ShapeDtypeStruct((count, NZ), F32)


def chip_pairs():
    return [[i, i + 1] for i in range(0, lax.axis_size("gx"), 2)]


def outward_x(distance):
    peers = lax.axis_size("gx")
    return [(i, (i + distance if i % 2 else i - distance) % peers) for i in range(peers)]


def column_pairs(distance, above):
    wide, tall = lax.axis_size("gx"), lax.axis_size("gy")
    return [
        [(x + above) * tall + y, (x + 1 - above) * tall + (y + distance) % tall]
        for x in range(0, wide, 2)
        for y in range(tall)
    ]


def swap_y(field, distance):
    route = []
    for low, high in column_pairs(distance, 0):
        route += [(low, high), (high, low)]
    return lax.ppermute(field, ("gx", "gy"), route)


def per_device(
    rel_pos,
    charges,
    block_cell,
    block_count,
    leaf_offsets,
    coarse_offsets,
    leaf_ops,
    coarse_ops,
    upward_ops,
    downward_ops,
):
    pos = rel_pos.reshape(3, BLKS, SLOT).transpose(1, 0, 2)
    charge = charges.reshape(NQ, BLKS, SLOT).transpose(1, 0, 2)
    cell = block_cell.reshape(1, BLKS)
    count = block_count.reshape(1, BLKS)
    upward = upward_ops.transpose(1, 0, 2)
    downward = downward_ops.transpose(1, 0, 2)
    index_row = pltpu.VMEM((1, LANES), jnp.int32)

    atoms = (pos, charge, cell, count, upward)
    own_field = call(
        moments_kernel,
        [rows(LEAF + PAIR)],
        [
            pltpu.VMEM((BLKS, 3, SLOT), F32),
            pltpu.VMEM((BLKS, NQ, SLOT), F32),
            pltpu.VMEM((1, BLKS), jnp.int32),
            pltpu.VMEM((1, BLKS), jnp.int32),
            pltpu.VMEM((NP, 8, NP), F32),
            pltpu.VMEM((NP, BLKS, SLOT), F32),
            pltpu.VMEM((NQ, BLKS, SLOT), F32),
            pltpu.VMEM((LEAF, LANES), F32),
            index_row,
            pltpu.VMEM((2 * PAD, PAD), F32),
            pltpu.SemaphoreType.DMA((5,)),
        ],
        [HBM] * 5,
        "moments",
        3,
    )(*[pltpu.with_memory_space_constraint(x, pltpu.HBM) for x in atoms])

    both = lax.all_gather(own_field, "gx", axis_index_groups=chip_pairs())
    near, parents = call(
        pair_kernel, [rows(2 * LEAF + PAIR), rows(PAIR)], [], [VMEM], "pair"
    )(both)
    beside = lax.ppermute(near, "gx", outward_x(1))
    beyond = lax.ppermute(parents, "gx", outward_x(3))
    leaf_k, coarse_k = call(
        tables_kernel,
        [
            jax.ShapeDtypeStruct((12 * PAD, DEPTH), BF16),
            jax.ShapeDtypeStruct((10 * PAD, DEPTH), BF16),
        ],
        [
            pltpu.VMEM((8, NZ), F32),
            pltpu.VMEM((TILES * PAD, 2 * NZ), F32),
        ],
        [VMEM] * 4,
        "tables",
        2,
    )(
        leaf_offsets.T,
        coarse_offsets.T,
        leaf_ops.transpose(1, 2, 0),
        coarse_ops.transpose(1, 2, 0),
    )
    side = call(join_kernel, [rows(2 * LEAF + 2 * PAIR)], [], [VMEM] * 2, "join")(beside, beyond)
    sides = lax.all_gather(side, "gx", axis_index_groups=chip_pairs())

    one, two, kept = call(
        translate_kernel,
        [rows(2 * LEAF + 2 * PAIR), rows(2 * LEAF + 2 * PAIR), rows(LEAF + 2 * PAIR)],
        [
            pltpu.VMEM((2, 6, LEAF, NZ), F32),
            pltpu.VMEM((2, 5, PAIR, NZ), F32),
            pltpu.VMEM((DEPTH, NQ * NZ), BF16),
            pltpu.VMEM((DEPTH, NQ * NZ), BF16),
            pltpu.VMEM((DEPTH, 2 * NZ), BF16),
            pltpu.VMEM((DEPTH, 2 * NZ), BF16),
        ],
        [VMEM] * 4,
        "translate",
        3,
    )(near, sides, leaf_k, coarse_k)

    one = swap_y(one, 1)
    two = swap_y(two, 2)
    relayed = call(relay_kernel, [rows(PAIR)], [], [VMEM] * 3, "relay")(kept, one, two)
    three = lax.all_gather(relayed, ("gx", "gy"), axis_index_groups=column_pairs(3, 1))
    basis = call(
        basis_kernel,
        [jax.ShapeDtypeStruct((NP, BLKS, SLOT), F32)],
        [],
        [VMEM] * 2,
        "basis",
    )(pos, kept)
    passed = call(exchange_kernel, [rows(LEAF + PAIR)], [], [VMEM] * 4, "exchange")(
        kept, one, two, three
    )
    last = lax.all_gather(passed, "gx", axis_index_groups=chip_pairs())

    potential = call(
        potential_kernel,
        [jax.ShapeDtypeStruct((BLKS, NQ, SLOT), F32)],
        [
            index_row,
            pltpu.VMEM((PAD, 2 * PAD), F32),
            pltpu.VMEM((NQ * PAD, LANES), F32),
            pltpu.VMEM((NQ, BLKS, SLOT), F32),
        ],
        [VMEM] * 8,
        "potential",
        3,
    )(kept, one, two, last, cell, count, downward, basis)
    return potential.transpose(1, 0, 2).reshape(NQ, BLKS * SLOT)


def solution(mesh):
    in_specs = (
        P(None, ("gx", "gy")),
        P(None, ("gx", "gy")),
        P(("gx", "gy")),
        P(("gx", "gy")),
        P(),
        P(),
        P(),
        P(),
        P(),
        P(),
    )
    out_specs = P(None, ("gx", "gy"))
    return jax.shard_map(
        per_device, mesh=mesh, in_specs=in_specs, out_specs=out_specs, check_vma=False
    )
```

```python
import math

import jax
import jax.numpy as jnp
from jax import lax
from jax.experimental import pallas as pl
from jax.experimental.pallas import tpu as pltpu
from jax.sharding import PartitionSpec as P

NQ = 4
NP = 25
NZ = 128
BLKS = 160
LANES = 256
EXTRA = BLKS - 128
SLOT = 128
CLS = 96
PAD = 32
LEAF = 104
PAIR = 56
GROUP = 32
TILES = 7
DEPTH = TILES * NZ
F32 = jnp.float32
BF16 = jnp.bfloat16

VMEM = pl.BlockSpec(memory_space=pltpu.VMEM)
HBM = pl.BlockSpec(memory_space=pltpu.HBM)


def harmonics(pos_x, pos_y, pos_z):
    point_x = 2.0 * pos_x
    point_y = 2.0 * pos_y
    point_z = 2.0 * pos_z
    radius_sq = point_x * point_x + point_y * point_y + point_z * point_z
    real_part = {(0, 0): jnp.ones_like(point_x)}
    imag_part = {}
    for degree in range(1, 5):
        lower_real = real_part[degree - 1, degree - 1]
        if degree == 1:
            real_part[1, 1] = point_x * 0.5
            imag_part[1, 1] = point_y * 0.5
        else:
            lower_imag = imag_part[degree - 1, degree - 1]
            scale = 1.0 / (2.0 * degree)
            real_part[degree, degree] = (point_x * lower_real - point_y * lower_imag) * scale
            imag_part[degree, degree] = (point_x * lower_imag + point_y * lower_real) * scale
        for azimuth in range(degree):
            scale = 1.0 / float((degree + azimuth) * (degree - azimuth))
            scale_z = ((2.0 * degree - 1.0) * scale) * point_z
            if degree == 1:
                real_part[1, 0] = scale_z
                continue
            next_real = scale_z * real_part[degree - 1, azimuth]
            if degree - 2 >= azimuth:
                scaled_sq = radius_sq * scale
                next_real = next_real - scaled_sq * real_part[degree - 2, azimuth]
            real_part[degree, azimuth] = next_real
            if azimuth > 0:
                next_imag = scale_z * imag_part[degree - 1, azimuth]
                if degree - 2 >= azimuth:
                    next_imag = next_imag - scaled_sq * imag_part[degree - 2, azimuth]
                imag_part[degree, azimuth] = next_imag
    rows_out = []
    for degree in range(5):
        rows_out.append(real_part[degree, 0] * float(math.factorial(degree)))
        for azimuth in range(1, degree + 1):
            factor = math.sqrt(math.factorial(degree + azimuth) * math.factorial(degree - azimuth))
            rows_out.append(real_part[degree, azimuth] * factor)
            rows_out.append(imag_part[degree, azimuth] * factor)
    return rows_out


def split(value):
    high = value.astype(BF16)
    low = (value - high.astype(F32)).astype(BF16)
    return high, low


def dot(left, right):
    return lax.dot_general(left, right, (((1,), (0,)), ((), ())), preferred_element_type=F32)


def exact_dot(left, right):
    high, low = split(left)
    top, rest = split(right)
    both = dot(jnp.concatenate([high, low], axis=0), top)
    return both[: left.shape[0]] + both[left.shape[0] :] + dot(high, rest)


def unpacked(field, channel, channels):
    zeros = jnp.zeros((PAD - NP, NZ), F32)
    return jnp.concatenate(
        [
            field[channel * 24 : channel * 24 + 24],
            field[channels * 24 + channel : channels * 24 + channel + 1],
            zeros,
        ],
        axis=0,
    )


def store_packed(ref, base, channel, channels, value):
    ref[base + channel * 24 : base + channel * 24 + 24, :] = value[:24]
    row = base + channels * 24 + channel
    ref[row : row + 1, :] = value[24:25]


def even_lanes(shape):
    return lax.broadcasted_iota(jnp.int32, shape, 1) % 2 == 0


def octant_rows(ref, octant):
    return ref.reshape(NP * 8, NP)[pl.ds(octant, NP, stride=8), :]


def parity(axis):
    return lax.rem(lax.axis_index(axis), 2)


def slots_down(tile):
    extra = tile[SLOT:, :]
    runs = [extra[:, g * EXTRA : (g + 1) * EXTRA] for g in range(4)]
    return jnp.concatenate([tile[:SLOT, :].T, jnp.concatenate(runs, axis=0).T], axis=0)


def blocks_down(tile):
    extra = tile[SLOT:, :].T
    runs = [extra[g * EXTRA : (g + 1) * EXTRA, :] for g in range(4)]
    return jnp.concatenate([tile[:SLOT, :].T, jnp.concatenate(runs, axis=1)], axis=0)


def spread_row(values, row):
    row[:, 0:SLOT] = values[:, 0:SLOT]
    for g in range(4):
        row[:, SLOT + g * EXTRA : SLOT + (g + 1) * EXTRA] = values[:, SLOT:BLKS]
    return row[...]


def member_t(cell_ref, row):
    cells = lax.broadcasted_iota(jnp.int32, (NZ, LANES), 0)
    return (cells == spread_row(cell_ref, row)).astype(F32)


def live_t(count_ref, row):
    counts = spread_row(count_ref, row)
    first = lax.broadcasted_iota(jnp.int32, (SLOT, SLOT), 0)
    run = lax.broadcasted_iota(jnp.int32, (EXTRA, SLOT), 1) // EXTRA
    second = lax.broadcasted_iota(jnp.int32, (EXTRA, SLOT), 0) + run * EXTRA
    return jnp.concatenate([first < counts[:, :SLOT], second < counts[:, SLOT:]], axis=0)


def moments_kernel(
    pos_in, charge_in, cell_in, count_in, upward_in, out, *scratch
):
    pos, charge, cell, count, upward, basis, weight, sums, row, ops, done = scratch
    copies = [
        pltpu.make_async_copy(source, target, done.at[n])
        for n, (source, target) in enumerate(
            (
                (pos_in, pos),
                (charge_in, charge),
                (cell_in, cell),
                (count_in, count),
                (upward_in, upward),
            )
        )
    ]
    for copy in copies:
        copy.start()
    copies[0].wait()
    coords = [slots_down(pos[:, d, :]) for d in range(3)]
    for j, value in enumerate(harmonics(*coords)):
        basis[j] = value
    for copy in copies[1:]:
        copy.wait()
    live = live_t(count, row)
    for q in range(NQ):
        weight[q] = jnp.where(live, slots_down(charge[:, q, :]), 0.0)
    sums[NQ * NP :, :] = jnp.zeros((LEAF - NQ * NP, LANES), F32)
    for j in range(NP):
        value = basis[j]
        for q in range(NQ):
            product = (weight[q] * value).reshape(BLKS // 8, 8, SLOT)
            at = q * 24 + j if j < 24 else 96 + q
            sums[at : at + 1, :SLOT] = jnp.sum(
                jnp.sum(product[: SLOT // 8], axis=0), axis=0, keepdims=True
            )
            sums[at : at + 1, SLOT:] = jnp.sum(
                jnp.sum(product[SLOT // 8 :], axis=0), axis=0, keepdims=True
            )
    member = member_t(cell, row).T.astype(BF16)
    high, low = split(sums[...])
    field = dot(high, member) + dot(low, member)
    out[0:LEAF, :] = field
    ops[...] = jnp.zeros_like(ops)
    octant = (parity("gx") * 2 + parity("gy")) * 2
    for c in range(2):
        ops[c * PAD : c * PAD + NP, 0:NP] = octant_rows(upward, octant + c)
    stacked = jnp.concatenate([unpacked(field, q, NQ) for q in range(NQ)], axis=1)
    raised = exact_dot(ops[...], stacked)
    out[LEAF : LEAF + PAIR, :] = jnp.zeros((PAIR, NZ), F32)
    even = even_lanes((PAD, NZ))
    for pair in range(2):
        first, second = [
            [raised[c * PAD : (c + 1) * PAD, q * NZ : (q + 1) * NZ] for c in range(2)]
            for q in (2 * pair, 2 * pair + 1)
        ]
        value = jnp.where(
            even,
            first[0] + pltpu.roll(first[1], NZ - 1, 1),
            pltpu.roll(second[0], 1, 1) + second[1],
        )
        store_packed(out, LEAF, pair, 2, value)


def tables_kernel(leaf_at, coarse_at, leaf_ops, coarse_ops, *refs):
    codes, left = refs[4:]
    toward = (1 - 2 * parity("gx")).astype(F32)
    lane = lax.broadcasted_iota(jnp.int32, (NZ, NZ), 1).astype(F32)
    for at, ops, outs, columns, reaches in (
        (leaf_at, leaf_ops, refs[0:2], 2, (0, 1, 2)),
        (coarse_at, coarse_ops, refs[2:4], 1, (0, 1, 2, -1, -2)),
    ):
        codes[...] = jnp.full((8, NZ), 99.0, F32)
        codes[0:3, 0:CLS] = at[...].astype(F32)
        turned = codes[...].T
        ahead = [-toward * turned[:, 1:2] == float(r) for r in reaches]
        places = []
        for own in (True, False):
            for t in range(columns):
                source = turned[:, 0:1] + float(2 + t)
                near = (source >= 2.0) & (source < float(2 + columns))
                if own:
                    chosen, column = near, source - 2.0
                else:
                    chosen = jnp.logical_not(near)
                    column = jnp.where(source < 2.0, source, source - float(columns))
                place = column * 8.0 + 3.0 - turned[:, 2:3]
                places.append(jnp.where(chosen, place, -1000.0))
        picks = []
        for part in range(4):
            blocks = []
            for place in places:
                found = lane == place + float(part * GROUP)
                blocks += [(found & row).astype(BF16) for row in ahead]
            picks.append(jnp.concatenate(blocks, axis=1))
        pick = jnp.concatenate(picks, axis=0)
        left[...] = jnp.zeros_like(left)
        for i in range(NP):
            row = (i // 4) * PAD
            col = (i % 4) * NZ
            left[row : row + NP, col : col + CLS] = ops[:, i, :]
        blocks = columns * len(reaches)
        for part, value in enumerate(split(left[...])):
            table = dot(value, pick).astype(BF16)
            for side, out in enumerate(outs):
                for tile in range(TILES):
                    for block in range(blocks):
                        row = (part * blocks + block) * PAD
                        col = (side * blocks + block) * NZ
                        out[row : row + PAD, tile * NZ : (tile + 1) * NZ] = table[
                            tile * PAD : (tile + 1) * PAD, col : col + NZ
                        ]


def pair_kernel(near, fields, parents):
    fields[0:LEAF, :] = near[0, 0:LEAF, :]
    fields[LEAF : 2 * LEAF, :] = near[1, 0:LEAF, :]
    total = near[0, LEAF:, :] + near[1, LEAF:, :]
    fields[2 * LEAF :, :] = total
    parents[...] = total


def join_kernel(fields, far, out):
    out[0 : 2 * LEAF + PAIR, :] = fields[...]
    out[2 * LEAF + PAIR :, :] = far[...]


def back(target, column, value, step):
    value = pltpu.roll(value, NZ - 3 * step, 1)
    top = value.astype(BF16).astype(F32)
    target[0, column] = top
    target[1, column] = value - top


def spread(source, columns, high, low, step):
    channels = high.shape[1] // NZ
    used = NP * GROUP
    for ref in (high, low):
        ref[used:, :] = jnp.zeros((DEPTH - used, ref.shape[1]), BF16)

    def turned(part, column, at):
        if column is None:
            return jnp.zeros((8, NZ), F32)
        value = jnp.broadcast_to(source[part, column, at : at + 1, :], (8, NZ))
        return pltpu.roll(value, 0, 1, stride=step, stride_axis=0)

    for i in range(NP):
        for two in range(2):
            base = i * GROUP + two * 16
            members = columns[2 * two : 2 * two + 2]
            for part, ref in enumerate((high, low)):
                if not members:
                    ref[base : base + 16, :] = jnp.zeros((16, ref.shape[1]), BF16)
                    continue
                for q in range(channels):
                    at = q * 24 + i if i < 24 else channels * 24 + q
                    value = jnp.concatenate(
                        [turned(part, column, at) for column in members], axis=0
                    )
                    ref[base : base + 16, q * NZ : (q + 1) * NZ] = value.astype(BF16)


def product(table, high, low):
    height = table.shape[0] // 2
    both = dot(table[...], high[...])
    return both[:height] + both[height:] + dot(table[0:height, :], low[...])


def own_kernel(near, leaf_k, coarse_k, leaf_out, coarse_out, *scratch):
    fields, parents, high, low, coarse_high, coarse_low = scratch
    back(parents, 0, near[2 * LEAF :, :], 2)
    for a in range(2):
        back(fields, a, near[a * LEAF : (a + 1) * LEAF, :], 1)
    spread(parents, [0, None], coarse_high, coarse_low, 2)
    spread(fields, [0, 1], high, low, 1)
    coarse_out[...] = product(coarse_k, coarse_high, coarse_low)
    leaf_out[...] = product(leaf_k, high, low)


def translate_kernel(sides, leaf_k, coarse_k, own_leaf, own_coarse, *refs):
    one_out, two_out, kept, fields, parents, high, low, coarse_high, coarse_low = refs
    core = parity("gx")

    def emit(ref, base, value, channels, rows):
        ref[base + channels * 25 : base + rows, :] = jnp.zeros((rows - channels * 25, NZ), F32)
        for q in range(channels):
            store_packed(ref, base, q, channels, value[:, q * NZ : (q + 1) * NZ])

    one, two = 2 * LEAF, 2 * LEAF + PAIR
    back(parents, 0, sides[0, two:, :], 2)
    back(parents, 1, sides[0, one:two, :], 2)
    back(parents, 2, sides[1, one:two, :], 2)
    back(parents, 3, sides[1, two:, :], 2)
    for a in range(2):
        back(fields, a, sides[0, a * LEAF : (a + 1) * LEAF, :], 1)
        back(fields, 2 + a, sides[1, a * LEAF : (a + 1) * LEAF, :], 1)
    spread(parents, [0, 1, 2, 3], coarse_high, coarse_low, 2)
    spread(fields, [0, 1, 2, 3], high, low, 1)
    result = product(coarse_k, coarse_high, coarse_low) + own_coarse[...]
    coarse = [result[b * PAD : (b + 1) * PAD] for b in range(5)]
    result = product(leaf_k, high, low) + own_leaf[...]
    blocks = [result[b * PAD : (b + 1) * PAD] for b in range(6)]
    for t in range(2):
        emit(one_out, t * LEAF, blocks[3 * t + 1], NQ, LEAF)
        emit(two_out, t * LEAF, blocks[3 * t + 2], NQ, LEAF)
    emit(kept, 0, jnp.where(core == 0, blocks[0], blocks[3]), NQ, LEAF)
    blocks = coarse
    outer = lax.rem(core + parity("gy"), 2) == 1
    emit(kept, LEAF, jnp.where(core == 0, blocks[0], 0.0), 2, PAIR)
    emit(kept, LEAF + PAIR, jnp.where(outer, blocks[3], blocks[4]), 2, PAIR)
    emit(one_out, 2 * LEAF, jnp.where(outer, blocks[1], blocks[0]), 2, PAIR)
    emit(one_out, 2 * LEAF + PAIR, blocks[2], 2, PAIR)
    emit(two_out, 2 * LEAF, blocks[1], 2, PAIR)
    emit(two_out, 2 * LEAF + PAIR, jnp.where(outer, 0.0, blocks[2]), 2, PAIR)


def relay_kernel(kept, one_in, two_in, out):
    relayed = one_in[2 * LEAF + PAIR :, :] + two_in[2 * LEAF + PAIR :, :]
    out[...] = kept[LEAF + PAIR :, :] + relayed


def exchange_kernel(kept, one_in, two_in, three_in, out):
    there = pl.ds(pl.multiple_of((1 - parity("gx")) * LEAF, 8), LEAF)
    out[0:LEAF, :] = one_in[there, :] + two_in[there, :]
    direct = pl.ds(2 * LEAF, PAIR)
    out[LEAF:, :] = kept[LEAF : LEAF + PAIR, :] + (
        one_in[direct, :] + two_in[direct, :] + three_in[parity("gx")]
    )


def basis_kernel(pos, after, basis):
    del after
    coords = [slots_down(pos[:, d, :]) for d in range(3)]
    for j, value in enumerate(harmonics(*coords)):
        basis[j] = value


def potential_kernel(
    kept, one_in, two_in, last, cell, count, downward, basis, out, row, ops, spread, result
):
    core = parity("gx")
    mine = pl.ds(pl.multiple_of(core * LEAF, 8), LEAF)
    leaf = kept[0:LEAF, :] + one_in[mine, :] + two_in[mine, :] + last[1 - core, 0:LEAF, :]
    coarse = last[0, LEAF:, :] + last[1, LEAF:, :]
    ops[...] = jnp.zeros_like(ops)
    octant = (parity("gx") * 2 + parity("gy")) * 2
    for c in range(2):
        ops[0:NP, c * PAD : c * PAD + NP] = octant_rows(downward, octant + c)
    even = even_lanes((PAD, NZ))
    columns = []
    for q in range(NQ):
        value = unpacked(coarse, q // 2, 2)
        if q % 2 == 0:
            down = [jnp.where(even, value, 0.0), jnp.where(even, 0.0, pltpu.roll(value, 1, 1))]
        else:
            down = [jnp.where(even, pltpu.roll(value, NZ - 1, 1), 0.0), jnp.where(even, 0.0, value)]
        columns.append(jnp.concatenate(down, axis=0))
    pushed = exact_dot(ops[0:PAD, :], jnp.concatenate(columns, axis=1))
    local = jnp.concatenate(
        [unpacked(leaf, q, NQ) + pushed[:, q * NZ : (q + 1) * NZ] for q in range(NQ)], axis=0
    )
    member = member_t(cell, row).astype(BF16)
    high, low = split(local)
    spread[...] = dot(high, member) + dot(low, member)
    live = live_t(count, row)
    for start, size, lane in ((0, 64, 0), (64, 64, 0), (SLOT, EXTRA, SLOT)):
        totals = [None] * NQ
        for j in range(NP):
            value = basis[j, start : start + size, :]
            for q in range(NQ):
                term = spread[q * PAD + j : q * PAD + j + 1, lane : lane + SLOT] * value
                totals[q] = term if j == 0 else totals[q] + term
        for q in range(NQ):
            result[q, start : start + size, :] = totals[q]
    for q in range(NQ):
        out[:, q, :] = blocks_down(jnp.where(live, result[q], 0.0))


def call(kernel, outs, scratch, specs, name, micros=1):
    return pl.pallas_call(
        kernel,
        out_shape=outs if len(outs) > 1 else outs[0],
        in_specs=specs,
        out_specs=[VMEM] * len(outs) if len(outs) > 1 else VMEM,
        scratch_shapes=scratch,
        cost_estimate=pl.CostEstimate(
            flops=int(micros * 1e9), bytes_accessed=1000000, transcendentals=0
        ),
        compiler_params=pltpu.CompilerParams(vmem_limit_bytes=24 * 1024 * 1024),
        name=name,
    )


def rows(count):
    return jax.ShapeDtypeStruct((count, NZ), F32)


def chip_pairs():
    return [[i, i + 1] for i in range(0, lax.axis_size("gx"), 2)]


def outward_x(distance):
    peers = lax.axis_size("gx")
    return [(i, (i + distance if i % 2 else i - distance) % peers) for i in range(peers)]


def column_pairs(distance, above):
    wide, tall = lax.axis_size("gx"), lax.axis_size("gy")
    return [
        [(x + above) * tall + y, (x + 1 - above) * tall + (y + distance) % tall]
        for x in range(0, wide, 2)
        for y in range(tall)
    ]


def swap_y(field, distance):
    route = []
    for low, high in column_pairs(distance, 0):
        route += [(low, high), (high, low)]
    return lax.ppermute(field, ("gx", "gy"), route)


def translation_scratch(leaf_columns, coarse_columns):
    return [
        pltpu.VMEM((2, leaf_columns, LEAF, NZ), F32),
        pltpu.VMEM((2, coarse_columns, PAIR, NZ), F32),
        pltpu.VMEM((DEPTH, NQ * NZ), BF16),
        pltpu.VMEM((DEPTH, NQ * NZ), BF16),
        pltpu.VMEM((DEPTH, 2 * NZ), BF16),
        pltpu.VMEM((DEPTH, 2 * NZ), BF16),
    ]


def per_device(
    rel_pos,
    charges,
    block_cell,
    block_count,
    leaf_offsets,
    coarse_offsets,
    leaf_ops,
    coarse_ops,
    upward_ops,
    downward_ops,
):
    pos = rel_pos.reshape(3, BLKS, SLOT).transpose(1, 0, 2)
    charge = charges.reshape(NQ, BLKS, SLOT).transpose(1, 0, 2)
    cell = block_cell.reshape(1, BLKS)
    count = block_count.reshape(1, BLKS)
    upward = upward_ops.transpose(1, 0, 2)
    downward = downward_ops.transpose(1, 0, 2)
    index_row = pltpu.VMEM((1, LANES), jnp.int32)

    atoms = (pos, charge, cell, count, upward)
    own_field = call(
        moments_kernel,
        [rows(LEAF + PAIR)],
        [
            pltpu.VMEM((BLKS, 3, SLOT), F32),
            pltpu.VMEM((BLKS, NQ, SLOT), F32),
            pltpu.VMEM((1, BLKS), jnp.int32),
            pltpu.VMEM((1, BLKS), jnp.int32),
            pltpu.VMEM((NP, 8, NP), F32),
            pltpu.VMEM((NP, BLKS, SLOT), F32),
            pltpu.VMEM((NQ, BLKS, SLOT), F32),
            pltpu.VMEM((LEAF, LANES), F32),
            index_row,
            pltpu.VMEM((2 * PAD, PAD), F32),
            pltpu.SemaphoreType.DMA((5,)),
        ],
        [HBM] * 5,
        "moments",
        3,
    )(*[pltpu.with_memory_space_constraint(x, pltpu.HBM) for x in atoms])

    both = lax.all_gather(own_field, "gx", axis_index_groups=chip_pairs())
    near, parents = call(
        pair_kernel, [rows(2 * LEAF + PAIR), rows(PAIR)], [], [VMEM], "pair"
    )(both)
    beside = lax.ppermute(near, "gx", outward_x(1))
    beyond = lax.ppermute(parents, "gx", outward_x(3))
    leaf_table = jax.ShapeDtypeStruct((12 * PAD, DEPTH), BF16)
    coarse_table = jax.ShapeDtypeStruct((10 * PAD, DEPTH), BF16)
    leaf_near, leaf_far, coarse_near, coarse_far = call(
        tables_kernel,
        [leaf_table, leaf_table, coarse_table, coarse_table],
        [pltpu.VMEM((8, NZ), F32), pltpu.VMEM((TILES * PAD, 4 * NZ), F32)],
        [VMEM] * 4,
        "tables",
        2,
    )(
        leaf_offsets.T,
        coarse_offsets.T,
        leaf_ops.transpose(1, 2, 0),
        coarse_ops.transpose(1, 2, 0),
    )
    own_leaf, own_coarse = call(
        own_kernel,
        [
            jax.ShapeDtypeStruct((6 * PAD, NQ * NZ), F32),
            jax.ShapeDtypeStruct((5 * PAD, 2 * NZ), F32),
        ],
        translation_scratch(2, 1),
        [VMEM] * 3,
        "own",
        2,
    )(near, leaf_near, coarse_near)
    side = call(join_kernel, [rows(2 * LEAF + 2 * PAIR)], [], [VMEM] * 2, "join")(beside, beyond)
    sides = lax.all_gather(side, "gx", axis_index_groups=chip_pairs())

    one, two, kept = call(
        translate_kernel,
        [rows(2 * LEAF + 2 * PAIR), rows(2 * LEAF + 2 * PAIR), rows(LEAF + 2 * PAIR)],
        translation_scratch(4, 4),
        [VMEM] * 5,
        "translate",
        3,
    )(sides, leaf_far, coarse_far, own_leaf, own_coarse)

    one = swap_y(one, 1)
    two = swap_y(two, 2)
    relayed = call(relay_kernel, [rows(PAIR)], [], [VMEM] * 3, "relay")(kept, one, two)
    three = lax.all_gather(relayed, ("gx", "gy"), axis_index_groups=column_pairs(3, 1))
    basis = call(
        basis_kernel,
        [jax.ShapeDtypeStruct((NP, BLKS, SLOT), F32)],
        [],
        [VMEM] * 2,
        "basis",
    )(pos, kept)
    passed = call(exchange_kernel, [rows(LEAF + PAIR)], [], [VMEM] * 4, "exchange")(
        kept, one, two, three
    )
    last = lax.all_gather(passed, "gx", axis_index_groups=chip_pairs())

    potential = call(
        potential_kernel,
        [jax.ShapeDtypeStruct((BLKS, NQ, SLOT), F32)],
        [
            index_row,
            pltpu.VMEM((PAD, 2 * PAD), F32),
            pltpu.VMEM((NQ * PAD, LANES), F32),
            pltpu.VMEM((NQ, BLKS, SLOT), F32),
        ],
        [VMEM] * 8,
        "potential",
        3,
    )(kept, one, two, last, cell, count, downward, basis)
    return potential.transpose(1, 0, 2).reshape(NQ, BLKS * SLOT)


def solution(mesh):
    in_specs = (
        P(None, ("gx", "gy")),
        P(None, ("gx", "gy")),
        P(("gx", "gy")),
        P(("gx", "gy")),
        P(),
        P(),
        P(),
        P(),
        P(),
        P(),
    )
    out_specs = P(None, ("gx", "gy"))
    return jax.shard_map(
        per_device, mesh=mesh, in_specs=in_specs, out_specs=out_specs, check_vma=False
    )
```

```python
import math

import jax
import jax.numpy as jnp
from jax import lax
from jax.experimental import pallas as pl
from jax.experimental.pallas import tpu as pltpu
from jax.sharding import PartitionSpec as P

NQ = 4
NP = 25
NZ = 128
BLKS = 160
LANES = 256
EXTRA = BLKS - 128
SLOT = 128
CLS = 96
PAD = 32
LEAF = 104
PAIR = 56
GROUP = 32
TILES = 7
DEPTH = TILES * NZ
F32 = jnp.float32
BF16 = jnp.bfloat16

VMEM = pl.BlockSpec(memory_space=pltpu.VMEM)
HBM = pl.BlockSpec(memory_space=pltpu.HBM)


def harmonics(pos_x, pos_y, pos_z):
    point_x = 2.0 * pos_x
    point_y = 2.0 * pos_y
    point_z = 2.0 * pos_z
    radius_sq = point_x * point_x + point_y * point_y + point_z * point_z
    real_part = {(0, 0): jnp.ones_like(point_x)}
    imag_part = {}
    for degree in range(1, 5):
        lower_real = real_part[degree - 1, degree - 1]
        if degree == 1:
            real_part[1, 1] = point_x * 0.5
            imag_part[1, 1] = point_y * 0.5
        else:
            lower_imag = imag_part[degree - 1, degree - 1]
            scale = 1.0 / (2.0 * degree)
            real_part[degree, degree] = (point_x * lower_real - point_y * lower_imag) * scale
            imag_part[degree, degree] = (point_x * lower_imag + point_y * lower_real) * scale
        for azimuth in range(degree):
            scale = 1.0 / float((degree + azimuth) * (degree - azimuth))
            scale_z = ((2.0 * degree - 1.0) * scale) * point_z
            if degree == 1:
                real_part[1, 0] = scale_z
                continue
            next_real = scale_z * real_part[degree - 1, azimuth]
            if degree - 2 >= azimuth:
                scaled_sq = radius_sq * scale
                next_real = next_real - scaled_sq * real_part[degree - 2, azimuth]
            real_part[degree, azimuth] = next_real
            if azimuth > 0:
                next_imag = scale_z * imag_part[degree - 1, azimuth]
                if degree - 2 >= azimuth:
                    next_imag = next_imag - scaled_sq * imag_part[degree - 2, azimuth]
                imag_part[degree, azimuth] = next_imag
    rows_out = []
    for degree in range(5):
        rows_out.append(real_part[degree, 0] * float(math.factorial(degree)))
        for azimuth in range(1, degree + 1):
            factor = math.sqrt(math.factorial(degree + azimuth) * math.factorial(degree - azimuth))
            rows_out.append(real_part[degree, azimuth] * factor)
            rows_out.append(imag_part[degree, azimuth] * factor)
    return rows_out


def split(value):
    high = value.astype(BF16)
    low = (value - high.astype(F32)).astype(BF16)
    return high, low


def dot(left, right):
    return lax.dot_general(left, right, (((1,), (0,)), ((), ())), preferred_element_type=F32)


def exact_dot(left, right):
    high, low = split(left)
    top, rest = split(right)
    both = dot(jnp.concatenate([high, low], axis=0), top)
    return both[: left.shape[0]] + both[left.shape[0] :] + dot(high, rest)


def unpacked(field, channel, channels):
    zeros = jnp.zeros((PAD - NP, NZ), F32)
    return jnp.concatenate(
        [
            field[channel * 24 : channel * 24 + 24],
            field[channels * 24 + channel : channels * 24 + channel + 1],
            zeros,
        ],
        axis=0,
    )


def store_packed(ref, base, channel, channels, value):
    ref[base + channel * 24 : base + channel * 24 + 24, :] = value[:24]
    row = base + channels * 24 + channel
    ref[row : row + 1, :] = value[24:25]


def even_lanes(shape):
    return lax.broadcasted_iota(jnp.int32, shape, 1) % 2 == 0


def octant_rows(ref, octant):
    return ref.reshape(NP * 8, NP)[pl.ds(octant, NP, stride=8), :]


def parity(axis):
    return lax.rem(lax.axis_index(axis), 2)


def slots_down(tile):
    extra = tile[SLOT:, :]
    runs = [extra[:, g * EXTRA : (g + 1) * EXTRA] for g in range(4)]
    return jnp.concatenate([tile[:SLOT, :].T, jnp.concatenate(runs, axis=0).T], axis=0)


def blocks_down(tile):
    extra = tile[SLOT:, :].T
    runs = [extra[g * EXTRA : (g + 1) * EXTRA, :] for g in range(4)]
    return jnp.concatenate([tile[:SLOT, :].T, jnp.concatenate(runs, axis=1)], axis=0)


def spread_row(values, row):
    row[:, 0:SLOT] = values[:, 0:SLOT]
    for g in range(4):
        row[:, SLOT + g * EXTRA : SLOT + (g + 1) * EXTRA] = values[:, SLOT:BLKS]
    return row[...]


def member_t(cell_ref, row):
    cells = lax.broadcasted_iota(jnp.int32, (NZ, LANES), 0)
    return (cells == spread_row(cell_ref, row)).astype(F32)


def live_t(count_ref, row):
    counts = spread_row(count_ref, row)
    first = lax.broadcasted_iota(jnp.int32, (SLOT, SLOT), 0)
    run = lax.broadcasted_iota(jnp.int32, (EXTRA, SLOT), 1) // EXTRA
    second = lax.broadcasted_iota(jnp.int32, (EXTRA, SLOT), 0) + run * EXTRA
    return jnp.concatenate([first < counts[:, :SLOT], second < counts[:, SLOT:]], axis=0)


def row_sums(parts):
    row = lax.broadcasted_iota(jnp.int32, parts[0].shape, 0)
    upper = row < 4
    parts = [
        jnp.where(upper, a, b) + pltpu.roll(jnp.where(upper, b, a), 4, 0)
        for a, b in zip(parts[:4], parts[4:])
    ]
    for distance in (2, 1):
        here = (row // distance) % 2 == 0
        half = len(parts) // 2
        parts = [
            jnp.where(here, a, b)
            + jnp.where(here, pltpu.roll(a, 8 - distance, 0), pltpu.roll(b, distance, 0))
            for a, b in zip(parts[:half], parts[half:])
        ]
    return parts[0]


def moments_kernel(
    pos_in, charge_in, cell_in, count_in, upward_in, out, *scratch
):
    pos, charge, cell, count, upward, basis, weight, row, ops, done = scratch
    copies = [
        pltpu.make_async_copy(source, target, done.at[n])
        for n, (source, target) in enumerate(
            (
                (pos_in, pos),
                (charge_in, charge),
                (cell_in, cell),
                (count_in, count),
                (upward_in, upward),
            )
        )
    ]
    for copy in copies:
        copy.start()
    copies[0].wait()
    coords = [slots_down(pos[:, d, :]) for d in range(3)]
    for j, value in enumerate(harmonics(*coords)):
        basis[j] = value
    for copy in copies[1:]:
        copy.wait()
    live = live_t(count, row)
    for q in range(NQ):
        weight[q] = jnp.where(live, slots_down(charge[:, q, :]), 0.0)

    def part(q, j):
        terms = weight[q] if j == 0 else weight[q] * basis[j]
        terms = terms.reshape(BLKS // 8, 8, SLOT)
        return jnp.concatenate(
            [jnp.sum(terms[: SLOT // 8], axis=0), jnp.sum(terms[SLOT // 8 :], axis=0)], axis=1
        )

    groups = [
        row_sums([part(q, j) for j in range(start, start + 8)])
        for q in range(NQ)
        for start in range(0, 24, 8)
    ]
    zeros = jnp.zeros((8, LANES), F32)
    groups.append(row_sums([part(q, 24) for q in range(NQ)] + [zeros] * 4))
    member = member_t(cell, row).T.astype(BF16)
    high, low = split(jnp.concatenate(groups, axis=0))
    field = dot(high, member) + dot(low, member)
    out[0:LEAF, :] = field
    ops[...] = jnp.zeros_like(ops)
    octant = (parity("gx") * 2 + parity("gy")) * 2
    for c in range(2):
        ops[c * PAD : c * PAD + NP, 0:NP] = octant_rows(upward, octant + c)
    stacked = jnp.concatenate([unpacked(field, q, NQ) for q in range(NQ)], axis=1)
    raised = exact_dot(ops[...], stacked)
    out[LEAF : LEAF + PAIR, :] = jnp.zeros((PAIR, NZ), F32)
    even = even_lanes((PAD, NZ))
    for pair in range(2):
        first, second = [
            [raised[c * PAD : (c + 1) * PAD, q * NZ : (q + 1) * NZ] for c in range(2)]
            for q in (2 * pair, 2 * pair + 1)
        ]
        value = jnp.where(
            even,
            first[0] + pltpu.roll(first[1], NZ - 1, 1),
            pltpu.roll(second[0], 1, 1) + second[1],
        )
        store_packed(out, LEAF, pair, 2, value)


def tables_kernel(leaf_at, coarse_at, leaf_ops, coarse_ops, *refs):
    codes, left = refs[4:]
    toward = (1 - 2 * parity("gx")).astype(F32)
    lane = lax.broadcasted_iota(jnp.int32, (NZ, NZ), 1).astype(F32)
    for at, ops, outs, columns, reaches in (
        (leaf_at, leaf_ops, refs[0:2], 2, (0, 1, 2)),
        (coarse_at, coarse_ops, refs[2:4], 1, (0, 1, 2, -1, -2)),
    ):
        codes[...] = jnp.full((8, NZ), 99.0, F32)
        codes[0:3, 0:CLS] = at[...].astype(F32)
        turned = codes[...].T
        ahead = [-toward * turned[:, 1:2] == float(r) for r in reaches]
        places = []
        for own in (True, False):
            for t in range(columns):
                source = turned[:, 0:1] + float(2 + t)
                near = (source >= 2.0) & (source < float(2 + columns))
                if own:
                    chosen, column = near, source - 2.0
                else:
                    chosen = jnp.logical_not(near)
                    column = jnp.where(source < 2.0, source, source - float(columns))
                place = column * 8.0 + 3.0 - turned[:, 2:3]
                places.append(jnp.where(chosen, place, -1000.0))
        picks = []
        for part in range(4):
            blocks = []
            for place in places:
                found = lane == place + float(part * GROUP)
                blocks += [(found & row).astype(BF16) for row in ahead]
            picks.append(jnp.concatenate(blocks, axis=1))
        pick = jnp.concatenate(picks, axis=0)
        left[...] = jnp.zeros_like(left)
        for i in range(NP):
            row = (i // 4) * PAD
            col = (i % 4) * NZ
            left[row : row + NP, col : col + CLS] = ops[:, i, :]
        blocks = columns * len(reaches)
        for part, value in enumerate(split(left[...])):
            table = dot(value, pick).astype(BF16)
            for side, out in enumerate(outs):
                for tile in range(TILES):
                    for block in range(blocks):
                        row = (part * blocks + block) * PAD
                        col = (side * blocks + block) * NZ
                        out[row : row + PAD, tile * NZ : (tile + 1) * NZ] = table[
                            tile * PAD : (tile + 1) * PAD, col : col + NZ
                        ]


def pair_kernel(near, fields, parents):
    fields[0:LEAF, :] = near[0, 0:LEAF, :]
    fields[LEAF : 2 * LEAF, :] = near[1, 0:LEAF, :]
    total = near[0, LEAF:, :] + near[1, LEAF:, :]
    fields[2 * LEAF :, :] = total
    parents[...] = total


def join_kernel(fields, far, out):
    out[0 : 2 * LEAF + PAIR, :] = fields[...]
    out[2 * LEAF + PAIR :, :] = far[...]


def back(target, column, value, step):
    value = pltpu.roll(value, NZ - 3 * step, 1)
    top = value.astype(BF16).astype(F32)
    target[0, column] = top
    target[1, column] = value - top


def spread(source, columns, high, low, step):
    channels = high.shape[1] // NZ
    used = NP * GROUP
    for ref in (high, low):
        ref[used:, :] = jnp.zeros((DEPTH - used, ref.shape[1]), BF16)

    def turned(part, column, at):
        if column is None:
            return jnp.zeros((8, NZ), F32)
        value = jnp.broadcast_to(source[part, column, at : at + 1, :], (8, NZ))
        return pltpu.roll(value, 0, 1, stride=step, stride_axis=0)

    for i in range(NP):
        for two in range(2):
            base = i * GROUP + two * 16
            members = columns[2 * two : 2 * two + 2]
            for part, ref in enumerate((high, low)):
                if not members:
                    ref[base : base + 16, :] = jnp.zeros((16, ref.shape[1]), BF16)
                    continue
                for q in range(channels):
                    at = q * 24 + i if i < 24 else channels * 24 + q
                    value = jnp.concatenate(
                        [turned(part, column, at) for column in members], axis=0
                    )
                    ref[base : base + 16, q * NZ : (q + 1) * NZ] = value.astype(BF16)


def product(table, high, low):
    height = table.shape[0] // 2
    both = dot(table[...], high[...])
    return both[:height] + both[height:] + dot(table[0:height, :], low[...])


def own_kernel(near, leaf_k, coarse_k, leaf_out, coarse_out, *scratch):
    fields, parents, high, low, coarse_high, coarse_low = scratch
    back(parents, 0, near[2 * LEAF :, :], 2)
    for a in range(2):
        back(fields, a, near[a * LEAF : (a + 1) * LEAF, :], 1)
    spread(parents, [0, None], coarse_high, coarse_low, 2)
    spread(fields, [0, 1], high, low, 1)
    coarse_out[...] = product(coarse_k, coarse_high, coarse_low)
    leaf_out[...] = product(leaf_k, high, low)


def translate_kernel(sides, leaf_k, coarse_k, own_leaf, own_coarse, *refs):
    one_out, two_out, kept, fields, parents, high, low, coarse_high, coarse_low = refs
    core = parity("gx")

    def emit(ref, base, value, channels, rows):
        ref[base + channels * 25 : base + rows, :] = jnp.zeros((rows - channels * 25, NZ), F32)
        for q in range(channels):
            store_packed(ref, base, q, channels, value[:, q * NZ : (q + 1) * NZ])

    one, two = 2 * LEAF, 2 * LEAF + PAIR
    back(parents, 0, sides[0, two:, :], 2)
    back(parents, 1, sides[0, one:two, :], 2)
    back(parents, 2, sides[1, one:two, :], 2)
    back(parents, 3, sides[1, two:, :], 2)
    for a in range(2):
        back(fields, a, sides[0, a * LEAF : (a + 1) * LEAF, :], 1)
        back(fields, 2 + a, sides[1, a * LEAF : (a + 1) * LEAF, :], 1)
    spread(parents, [0, 1, 2, 3], coarse_high, coarse_low, 2)
    spread(fields, [0, 1, 2, 3], high, low, 1)
    result = product(coarse_k, coarse_high, coarse_low) + own_coarse[...]
    coarse = [result[b * PAD : (b + 1) * PAD] for b in range(5)]
    result = product(leaf_k, high, low) + own_leaf[...]
    blocks = [result[b * PAD : (b + 1) * PAD] for b in range(6)]
    for t in range(2):
        emit(one_out, t * LEAF, blocks[3 * t + 1], NQ, LEAF)
        emit(two_out, t * LEAF, blocks[3 * t + 2], NQ, LEAF)
    emit(kept, 0, jnp.where(core == 0, blocks[0], blocks[3]), NQ, LEAF)
    blocks = coarse
    outer = lax.rem(core + parity("gy"), 2) == 1
    emit(kept, LEAF, jnp.where(core == 0, blocks[0], 0.0), 2, PAIR)
    emit(kept, LEAF + PAIR, jnp.where(outer, blocks[3], blocks[4]), 2, PAIR)
    emit(one_out, 2 * LEAF, jnp.where(outer, blocks[1], blocks[0]), 2, PAIR)
    emit(one_out, 2 * LEAF + PAIR, blocks[2], 2, PAIR)
    emit(two_out, 2 * LEAF, blocks[1], 2, PAIR)
    emit(two_out, 2 * LEAF + PAIR, jnp.where(outer, 0.0, blocks[2]), 2, PAIR)


def relay_kernel(kept, one_in, two_in, out):
    relayed = one_in[2 * LEAF + PAIR :, :] + two_in[2 * LEAF + PAIR :, :]
    out[...] = kept[LEAF + PAIR :, :] + relayed


def exchange_kernel(kept, one_in, two_in, three_in, out):
    there = pl.ds(pl.multiple_of((1 - parity("gx")) * LEAF, 8), LEAF)
    out[0:LEAF, :] = one_in[there, :] + two_in[there, :]
    direct = pl.ds(2 * LEAF, PAIR)
    out[LEAF:, :] = kept[LEAF : LEAF + PAIR, :] + (
        one_in[direct, :] + two_in[direct, :] + three_in[parity("gx")]
    )


def basis_kernel(pos, cell, count, after, basis, live, member, row):
    del after
    coords = [slots_down(pos[:, d, :]) for d in range(3)]
    for j, value in enumerate(harmonics(*coords)):
        basis[j] = value
    member[...] = member_t(cell, row).astype(BF16)
    live[...] = live_t(count, row).astype(F32)


def potential_kernel(
    kept, one_in, two_in, last, downward, basis, live, member, out, ops, spread, result
):
    core = parity("gx")
    mine = pl.ds(pl.multiple_of(core * LEAF, 8), LEAF)
    leaf = kept[0:LEAF, :] + one_in[mine, :] + two_in[mine, :] + last[1 - core, 0:LEAF, :]
    coarse = last[0, LEAF:, :] + last[1, LEAF:, :]
    ops[...] = jnp.zeros_like(ops)
    octant = (parity("gx") * 2 + parity("gy")) * 2
    for c in range(2):
        ops[0:NP, c * PAD : c * PAD + NP] = octant_rows(downward, octant + c)
    even = even_lanes((PAD, NZ))
    columns = []
    for q in range(NQ):
        value = unpacked(coarse, q // 2, 2)
        if q % 2 == 0:
            down = [jnp.where(even, value, 0.0), jnp.where(even, 0.0, pltpu.roll(value, 1, 1))]
        else:
            down = [jnp.where(even, pltpu.roll(value, NZ - 1, 1), 0.0), jnp.where(even, 0.0, value)]
        columns.append(jnp.concatenate(down, axis=0))
    pushed = exact_dot(ops[0:PAD, :], jnp.concatenate(columns, axis=1))
    local = jnp.concatenate(
        [unpacked(leaf, q, NQ) + pushed[:, q * NZ : (q + 1) * NZ] for q in range(NQ)], axis=0
    )
    high, low = split(local)
    spread[...] = dot(high, member[...]) + dot(low, member[...])
    for start, size, lane in ((0, 64, 0), (64, 64, 0), (SLOT, EXTRA, SLOT)):
        totals = [None] * NQ
        for j in range(NP):
            value = basis[j, start : start + size, :]
            for q in range(NQ):
                term = spread[q * PAD + j : q * PAD + j + 1, lane : lane + SLOT]
                totals[q] = term if j == 0 else totals[q] + term * value
        for q in range(NQ):
            result[q, start : start + size, :] = totals[q]
    for q in range(NQ):
        out[:, q, :] = blocks_down(jnp.where(live[...] > 0.0, result[q], 0.0))


def call(kernel, outs, scratch, specs, name, micros=1):
    return pl.pallas_call(
        kernel,
        out_shape=outs if len(outs) > 1 else outs[0],
        in_specs=specs,
        out_specs=[VMEM] * len(outs) if len(outs) > 1 else VMEM,
        scratch_shapes=scratch,
        cost_estimate=pl.CostEstimate(
            flops=int(micros * 1e9), bytes_accessed=1000000, transcendentals=0
        ),
        compiler_params=pltpu.CompilerParams(vmem_limit_bytes=24 * 1024 * 1024),
        name=name,
    )


def rows(count):
    return jax.ShapeDtypeStruct((count, NZ), F32)


def chip_pairs():
    return [[i, i + 1] for i in range(0, lax.axis_size("gx"), 2)]


def outward_x(distance):
    peers = lax.axis_size("gx")
    return [(i, (i + distance if i % 2 else i - distance) % peers) for i in range(peers)]


def column_pairs(distance, above):
    wide, tall = lax.axis_size("gx"), lax.axis_size("gy")
    return [
        [(x + above) * tall + y, (x + 1 - above) * tall + (y + distance) % tall]
        for x in range(0, wide, 2)
        for y in range(tall)
    ]


def swap_y(field, distance):
    route = []
    for low, high in column_pairs(distance, 0):
        route += [(low, high), (high, low)]
    return lax.ppermute(field, ("gx", "gy"), route)


def translation_scratch(leaf_columns, coarse_columns):
    return [
        pltpu.VMEM((2, leaf_columns, LEAF, NZ), F32),
        pltpu.VMEM((2, coarse_columns, PAIR, NZ), F32),
        pltpu.VMEM((DEPTH, NQ * NZ), BF16),
        pltpu.VMEM((DEPTH, NQ * NZ), BF16),
        pltpu.VMEM((DEPTH, 2 * NZ), BF16),
        pltpu.VMEM((DEPTH, 2 * NZ), BF16),
    ]


def per_device(
    rel_pos,
    charges,
    block_cell,
    block_count,
    leaf_offsets,
    coarse_offsets,
    leaf_ops,
    coarse_ops,
    upward_ops,
    downward_ops,
):
    pos = rel_pos.reshape(3, BLKS, SLOT).transpose(1, 0, 2)
    charge = charges.reshape(NQ, BLKS, SLOT).transpose(1, 0, 2)
    cell = block_cell.reshape(1, BLKS)
    count = block_count.reshape(1, BLKS)
    upward = upward_ops.transpose(1, 0, 2)
    downward = downward_ops.transpose(1, 0, 2)
    index_row = pltpu.VMEM((1, LANES), jnp.int32)

    atoms = (pos, charge, cell, count, upward)
    own_field = call(
        moments_kernel,
        [rows(LEAF + PAIR)],
        [
            pltpu.VMEM((BLKS, 3, SLOT), F32),
            pltpu.VMEM((BLKS, NQ, SLOT), F32),
            pltpu.VMEM((1, BLKS), jnp.int32),
            pltpu.VMEM((1, BLKS), jnp.int32),
            pltpu.VMEM((NP, 8, NP), F32),
            pltpu.VMEM((NP, BLKS, SLOT), F32),
            pltpu.VMEM((NQ, BLKS, SLOT), F32),
            index_row,
            pltpu.VMEM((2 * PAD, PAD), F32),
            pltpu.SemaphoreType.DMA((5,)),
        ],
        [HBM] * 5,
        "moments",
        3,
    )(*[pltpu.with_memory_space_constraint(x, pltpu.HBM) for x in atoms])

    both = lax.all_gather(own_field, "gx", axis_index_groups=chip_pairs())
    near, parents = call(
        pair_kernel, [rows(2 * LEAF + PAIR), rows(PAIR)], [], [VMEM], "pair"
    )(both)
    beside = lax.ppermute(near, "gx", outward_x(1))
    beyond = lax.ppermute(parents, "gx", outward_x(3))
    leaf_table = jax.ShapeDtypeStruct((12 * PAD, DEPTH), BF16)
    coarse_table = jax.ShapeDtypeStruct((10 * PAD, DEPTH), BF16)
    leaf_near, leaf_far, coarse_near, coarse_far = call(
        tables_kernel,
        [leaf_table, leaf_table, coarse_table, coarse_table],
        [pltpu.VMEM((8, NZ), F32), pltpu.VMEM((TILES * PAD, 4 * NZ), F32)],
        [VMEM] * 4,
        "tables",
        2,
    )(
        leaf_offsets.T,
        coarse_offsets.T,
        leaf_ops.transpose(1, 2, 0),
        coarse_ops.transpose(1, 2, 0),
    )
    own_leaf, own_coarse = call(
        own_kernel,
        [
            jax.ShapeDtypeStruct((6 * PAD, NQ * NZ), F32),
            jax.ShapeDtypeStruct((5 * PAD, 2 * NZ), F32),
        ],
        translation_scratch(2, 1),
        [VMEM] * 3,
        "own",
        2,
    )(near, leaf_near, coarse_near)
    side = call(join_kernel, [rows(2 * LEAF + 2 * PAIR)], [], [VMEM] * 2, "join")(beside, beyond)
    sides = lax.all_gather(side, "gx", axis_index_groups=chip_pairs())

    one, two, kept = call(
        translate_kernel,
        [rows(2 * LEAF + 2 * PAIR), rows(2 * LEAF + 2 * PAIR), rows(LEAF + 2 * PAIR)],
        translation_scratch(4, 4),
        [VMEM] * 5,
        "translate",
        3,
    )(sides, leaf_far, coarse_far, own_leaf, own_coarse)

    one = swap_y(one, 1)
    two = swap_y(two, 2)
    relayed = call(relay_kernel, [rows(PAIR)], [], [VMEM] * 3, "relay")(kept, one, two)
    three = lax.all_gather(relayed, ("gx", "gy"), axis_index_groups=column_pairs(3, 1))
    basis, live, member = call(
        basis_kernel,
        [
            jax.ShapeDtypeStruct((NP, BLKS, SLOT), F32),
            jax.ShapeDtypeStruct((BLKS, SLOT), F32),
            jax.ShapeDtypeStruct((NZ, LANES), BF16),
        ],
        [index_row],
        [VMEM] * 4,
        "basis",
    )(pos, cell, count, kept)
    passed = call(exchange_kernel, [rows(LEAF + PAIR)], [], [VMEM] * 4, "exchange")(
        kept, one, two, three
    )
    last = lax.all_gather(passed, "gx", axis_index_groups=chip_pairs())

    potential = call(
        potential_kernel,
        [jax.ShapeDtypeStruct((BLKS, NQ, SLOT), F32)],
        [
            pltpu.VMEM((PAD, 2 * PAD), F32),
            pltpu.VMEM((NQ * PAD, LANES), F32),
            pltpu.VMEM((NQ, BLKS, SLOT), F32),
        ],
        [VMEM] * 8,
        "potential",
        3,
    )(kept, one, two, last, downward, basis, live, member)
    return potential.transpose(1, 0, 2).reshape(NQ, BLKS * SLOT)


def solution(mesh):
    in_specs = (
        P(None, ("gx", "gy")),
        P(None, ("gx", "gy")),
        P(("gx", "gy")),
        P(("gx", "gy")),
        P(),
        P(),
        P(),
        P(),
        P(),
        P(),
    )
    out_specs = P(None, ("gx", "gy"))
    return jax.shard_map(
        per_device, mesh=mesh, in_specs=in_specs, out_specs=out_specs, check_vma=False
    )
```

```python
import math

import jax
import jax.numpy as jnp
from jax import lax
from jax.experimental import pallas as pl
from jax.experimental.pallas import tpu as pltpu
from jax.sharding import PartitionSpec as P

NQ = 4
NP = 25
NZ = 128
BLKS = 160
LANES = 256
EXTRA = BLKS - 128
SLOT = 128
CLS = 96
PAD = 32
LEAF = 104
PAIR = 56
GROUP = 32
TILES = 7
DEPTH = TILES * NZ
F32 = jnp.float32
BF16 = jnp.bfloat16

VMEM = pl.BlockSpec(memory_space=pltpu.VMEM)
HBM = pl.BlockSpec(memory_space=pltpu.HBM)


def harmonics(pos_x, pos_y, pos_z):
    point_x = 2.0 * pos_x
    point_y = 2.0 * pos_y
    point_z = 2.0 * pos_z
    radius_sq = point_x * point_x + point_y * point_y + point_z * point_z
    real_part = {(0, 0): jnp.ones_like(point_x)}
    imag_part = {}
    for degree in range(1, 5):
        lower_real = real_part[degree - 1, degree - 1]
        if degree == 1:
            real_part[1, 1] = point_x * 0.5
            imag_part[1, 1] = point_y * 0.5
        else:
            lower_imag = imag_part[degree - 1, degree - 1]
            scale = 1.0 / (2.0 * degree)
            real_part[degree, degree] = (point_x * lower_real - point_y * lower_imag) * scale
            imag_part[degree, degree] = (point_x * lower_imag + point_y * lower_real) * scale
        for azimuth in range(degree):
            scale = 1.0 / float((degree + azimuth) * (degree - azimuth))
            scale_z = ((2.0 * degree - 1.0) * scale) * point_z
            if degree == 1:
                real_part[1, 0] = scale_z
                continue
            next_real = scale_z * real_part[degree - 1, azimuth]
            if degree - 2 >= azimuth:
                scaled_sq = radius_sq * scale
                next_real = next_real - scaled_sq * real_part[degree - 2, azimuth]
            real_part[degree, azimuth] = next_real
            if azimuth > 0:
                next_imag = scale_z * imag_part[degree - 1, azimuth]
                if degree - 2 >= azimuth:
                    next_imag = next_imag - scaled_sq * imag_part[degree - 2, azimuth]
                imag_part[degree, azimuth] = next_imag
    rows_out = []
    for degree in range(5):
        rows_out.append(real_part[degree, 0] * float(math.factorial(degree)))
        for azimuth in range(1, degree + 1):
            factor = math.sqrt(math.factorial(degree + azimuth) * math.factorial(degree - azimuth))
            rows_out.append(real_part[degree, azimuth] * factor)
            rows_out.append(imag_part[degree, azimuth] * factor)
    return rows_out


def split(value):
    high = value.astype(BF16)
    low = (value - high.astype(F32)).astype(BF16)
    return high, low


def dot(left, right):
    return lax.dot_general(left, right, (((1,), (0,)), ((), ())), preferred_element_type=F32)


def exact_dot(left, right):
    high, low = split(left)
    top, rest = split(right)
    both = dot(jnp.concatenate([high, low], axis=0), top)
    return both[: left.shape[0]] + both[left.shape[0] :] + dot(high, rest)


def unpacked(field, channel, channels):
    zeros = jnp.zeros((PAD - NP, NZ), F32)
    return jnp.concatenate(
        [
            field[channel * 24 : channel * 24 + 24],
            field[channels * 24 + channel : channels * 24 + channel + 1],
            zeros,
        ],
        axis=0,
    )


def store_packed(ref, base, channel, channels, value):
    ref[base + channel * 24 : base + channel * 24 + 24, :] = value[:24]
    row = base + channels * 24 + channel
    ref[row : row + 1, :] = value[24:25]


def even_lanes(shape):
    return lax.broadcasted_iota(jnp.int32, shape, 1) % 2 == 0


def octant_rows(ref, octant):
    return ref.reshape(NP * 8, NP)[pl.ds(octant, NP, stride=8), :]


def parity(axis):
    return lax.rem(lax.axis_index(axis), 2)


def slots_down(tile):
    extra = tile[SLOT:, :]
    runs = [extra[:, g * EXTRA : (g + 1) * EXTRA] for g in range(4)]
    return jnp.concatenate([tile[:SLOT, :].T, jnp.concatenate(runs, axis=0).T], axis=0)


def spread_row(values, row):
    row[:, 0:SLOT] = values[:, 0:SLOT]
    for g in range(4):
        row[:, SLOT + g * EXTRA : SLOT + (g + 1) * EXTRA] = values[:, SLOT:BLKS]
    return row[...]


def member_t(cell_ref, row):
    cells = lax.broadcasted_iota(jnp.int32, (NZ, LANES), 0)
    return (cells == spread_row(cell_ref, row)).astype(F32)


def live_t(count_ref, row):
    counts = spread_row(count_ref, row)
    first = lax.broadcasted_iota(jnp.int32, (SLOT, SLOT), 0)
    run = lax.broadcasted_iota(jnp.int32, (EXTRA, SLOT), 1) // EXTRA
    second = lax.broadcasted_iota(jnp.int32, (EXTRA, SLOT), 0) + run * EXTRA
    return jnp.concatenate([first < counts[:, :SLOT], second < counts[:, SLOT:]], axis=0)


def row_sums(parts):
    row = lax.broadcasted_iota(jnp.int32, parts[0].shape, 0)
    upper = row < 4
    parts = [
        jnp.where(upper, a, b) + pltpu.roll(jnp.where(upper, b, a), 4, 0)
        for a, b in zip(parts[:4], parts[4:])
    ]
    for distance in (2, 1):
        here = (row // distance) % 2 == 0
        half = len(parts) // 2
        parts = [
            jnp.where(here, a, b)
            + jnp.where(here, pltpu.roll(a, 8 - distance, 0), pltpu.roll(b, distance, 0))
            for a, b in zip(parts[:half], parts[half:])
        ]
    return parts[0]


def moments_kernel(
    pos_in, charge_in, cell_in, count_in, upward_in, out, *scratch
):
    pos, charge, cell, count, upward, basis, weight, row, ops, done = scratch
    copies = [
        pltpu.make_async_copy(source, target, done.at[n])
        for n, (source, target) in enumerate(
            (
                (pos_in, pos),
                (charge_in, charge),
                (cell_in, cell),
                (count_in, count),
                (upward_in, upward),
            )
        )
    ]
    for copy in copies:
        copy.start()
    copies[0].wait()
    coords = [slots_down(pos[:, d, :]) for d in range(3)]
    for j, value in enumerate(harmonics(*coords)):
        basis[j] = value
    for copy in copies[1:]:
        copy.wait()
    live = live_t(count, row)
    for q in range(NQ):
        weight[q] = jnp.where(live, slots_down(charge[:, q, :]), 0.0)

    def part(q, j):
        terms = weight[q] if j == 0 else weight[q] * basis[j]
        terms = terms.reshape(BLKS // 8, 8, SLOT)
        return jnp.concatenate(
            [jnp.sum(terms[: SLOT // 8], axis=0), jnp.sum(terms[SLOT // 8 :], axis=0)], axis=1
        )

    groups = [
        row_sums([part(q, j) for j in range(start, start + 8)])
        for q in range(NQ)
        for start in range(0, 24, 8)
    ]
    zeros = jnp.zeros((8, LANES), F32)
    groups.append(row_sums([part(q, 24) for q in range(NQ)] + [zeros] * 4))
    member = member_t(cell, row).T.astype(BF16)
    high, low = split(jnp.concatenate(groups, axis=0))
    field = dot(high, member) + dot(low, member)
    out[0:LEAF, :] = field
    ops[...] = jnp.zeros_like(ops)
    octant = (parity("gx") * 2 + parity("gy")) * 2
    for c in range(2):
        ops[c * PAD : c * PAD + NP, 0:NP] = octant_rows(upward, octant + c)
    stacked = jnp.concatenate([unpacked(field, q, NQ) for q in range(NQ)], axis=1)
    raised = exact_dot(ops[...], stacked)
    out[LEAF : LEAF + PAIR, :] = jnp.zeros((PAIR, NZ), F32)
    even = even_lanes((PAD, NZ))
    for pair in range(2):
        first, second = [
            [raised[c * PAD : (c + 1) * PAD, q * NZ : (q + 1) * NZ] for c in range(2)]
            for q in (2 * pair, 2 * pair + 1)
        ]
        value = jnp.where(
            even,
            first[0] + pltpu.roll(first[1], NZ - 1, 1),
            pltpu.roll(second[0], 1, 1) + second[1],
        )
        store_packed(out, LEAF, pair, 2, value)


def tables_kernel(leaf_at, coarse_at, leaf_ops, coarse_ops, *refs):
    codes, left = refs[4:]
    toward = (1 - 2 * parity("gx")).astype(F32)
    lane = lax.broadcasted_iota(jnp.int32, (NZ, NZ), 1).astype(F32)
    for at, ops, outs, columns, reaches in (
        (leaf_at, leaf_ops, refs[0:2], 2, (0, 1, 2)),
        (coarse_at, coarse_ops, refs[2:4], 1, (0, 1, 2, -1, -2)),
    ):
        codes[...] = jnp.full((8, NZ), 99.0, F32)
        codes[0:3, 0:CLS] = at[...].astype(F32)
        turned = codes[...].T
        ahead = [-toward * turned[:, 1:2] == float(r) for r in reaches]
        places = []
        for own in (True, False):
            for t in range(columns):
                source = turned[:, 0:1] + float(2 + t)
                near = (source >= 2.0) & (source < float(2 + columns))
                if own:
                    chosen, column = near, source - 2.0
                else:
                    chosen = jnp.logical_not(near)
                    column = jnp.where(source < 2.0, source, source - float(columns))
                place = column * 8.0 + 3.0 - turned[:, 2:3]
                places.append(jnp.where(chosen, place, -1000.0))
        picks = []
        for part in range(4):
            blocks = []
            for place in places:
                found = lane == place + float(part * GROUP)
                blocks += [(found & row).astype(BF16) for row in ahead]
            picks.append(jnp.concatenate(blocks, axis=1))
        pick = jnp.concatenate(picks, axis=0)
        left[...] = jnp.zeros_like(left)
        for i in range(NP):
            row = (i // 4) * PAD
            col = (i % 4) * NZ
            left[row : row + NP, col : col + CLS] = ops[:, i, :]
        blocks = columns * len(reaches)
        for part, value in enumerate(split(left[...])):
            table = dot(value, pick).astype(BF16)
            for side, out in enumerate(outs):
                for tile in range(TILES):
                    for block in range(blocks):
                        row = (part * blocks + block) * PAD
                        col = (side * blocks + block) * NZ
                        out[row : row + PAD, tile * NZ : (tile + 1) * NZ] = table[
                            tile * PAD : (tile + 1) * PAD, col : col + NZ
                        ]


def pair_kernel(near, fields, parents):
    fields[0:LEAF, :] = near[0, 0:LEAF, :]
    fields[LEAF : 2 * LEAF, :] = near[1, 0:LEAF, :]
    total = near[0, LEAF:, :] + near[1, LEAF:, :]
    fields[2 * LEAF :, :] = total
    parents[...] = total


def join_kernel(fields, far, out):
    out[0 : 2 * LEAF + PAIR, :] = fields[...]
    out[2 * LEAF + PAIR :, :] = far[...]


def back(target, column, value, step):
    value = pltpu.roll(value, NZ - 3 * step, 1)
    top = value.astype(BF16).astype(F32)
    target[0, column] = top
    target[1, column] = value - top


def spread(source, columns, high, low, step):
    channels = high.shape[1] // NZ
    used = NP * GROUP
    for ref in (high, low):
        ref[used:, :] = jnp.zeros((DEPTH - used, ref.shape[1]), BF16)

    def turned(part, column, at):
        if column is None:
            return jnp.zeros((8, NZ), F32)
        value = jnp.broadcast_to(source[part, column, at : at + 1, :], (8, NZ))
        return pltpu.roll(value, 0, 1, stride=step, stride_axis=0)

    for i in range(NP):
        for two in range(2):
            base = i * GROUP + two * 16
            members = columns[2 * two : 2 * two + 2]
            for part, ref in enumerate((high, low)):
                if not members:
                    ref[base : base + 16, :] = jnp.zeros((16, ref.shape[1]), BF16)
                    continue
                for q in range(channels):
                    at = q * 24 + i if i < 24 else channels * 24 + q
                    value = jnp.concatenate(
                        [turned(part, column, at) for column in members], axis=0
                    )
                    ref[base : base + 16, q * NZ : (q + 1) * NZ] = value.astype(BF16)


def product(table, high, low):
    height = table.shape[0] // 2
    both = dot(table[...], high[...])
    return both[:height] + both[height:] + dot(table[0:height, :], low[...])


def own_kernel(near, leaf_k, coarse_k, leaf_out, coarse_out, *scratch):
    fields, parents, high, low, coarse_high, coarse_low = scratch
    back(parents, 0, near[2 * LEAF :, :], 2)
    for a in range(2):
        back(fields, a, near[a * LEAF : (a + 1) * LEAF, :], 1)
    spread(parents, [0, None], coarse_high, coarse_low, 2)
    spread(fields, [0, 1], high, low, 1)
    coarse_out[...] = product(coarse_k, coarse_high, coarse_low)
    leaf_out[...] = product(leaf_k, high, low)


def translate_kernel(sides, leaf_k, coarse_k, own_leaf, own_coarse, *refs):
    one_out, two_out, kept, fields, parents, high, low, coarse_high, coarse_low = refs
    core = parity("gx")

    def emit(ref, base, value, channels, rows):
        ref[base + channels * 25 : base + rows, :] = jnp.zeros((rows - channels * 25, NZ), F32)
        for q in range(channels):
            store_packed(ref, base, q, channels, value[:, q * NZ : (q + 1) * NZ])

    one, two = 2 * LEAF, 2 * LEAF + PAIR
    back(parents, 0, sides[0, two:, :], 2)
    back(parents, 1, sides[0, one:two, :], 2)
    back(parents, 2, sides[1, one:two, :], 2)
    back(parents, 3, sides[1, two:, :], 2)
    for a in range(2):
        back(fields, a, sides[0, a * LEAF : (a + 1) * LEAF, :], 1)
        back(fields, 2 + a, sides[1, a * LEAF : (a + 1) * LEAF, :], 1)
    spread(parents, [0, 1, 2, 3], coarse_high, coarse_low, 2)
    spread(fields, [0, 1, 2, 3], high, low, 1)
    result = product(coarse_k, coarse_high, coarse_low) + own_coarse[...]
    coarse = [result[b * PAD : (b + 1) * PAD] for b in range(5)]
    result = product(leaf_k, high, low) + own_leaf[...]
    blocks = [result[b * PAD : (b + 1) * PAD] for b in range(6)]
    for t in range(2):
        emit(one_out, t * LEAF, blocks[3 * t + 1], NQ, LEAF)
        emit(two_out, t * LEAF, blocks[3 * t + 2], NQ, LEAF)
    emit(kept, 0, jnp.where(core == 0, blocks[0], blocks[3]), NQ, LEAF)
    blocks = coarse
    outer = lax.rem(core + parity("gy"), 2) == 1
    emit(kept, LEAF, jnp.where(core == 0, blocks[0], 0.0), 2, PAIR)
    emit(kept, LEAF + PAIR, jnp.where(outer, blocks[3], blocks[4]), 2, PAIR)
    emit(one_out, 2 * LEAF, jnp.where(outer, blocks[1], blocks[0]), 2, PAIR)
    emit(one_out, 2 * LEAF + PAIR, blocks[2], 2, PAIR)
    emit(two_out, 2 * LEAF, blocks[1], 2, PAIR)
    emit(two_out, 2 * LEAF + PAIR, jnp.where(outer, 0.0, blocks[2]), 2, PAIR)


def relay_kernel(kept, one_in, two_in, out):
    relayed = one_in[2 * LEAF + PAIR :, :] + two_in[2 * LEAF + PAIR :, :]
    out[...] = kept[LEAF + PAIR :, :] + relayed


def exchange_kernel(kept, one_in, two_in, three_in, out):
    there = pl.ds(pl.multiple_of((1 - parity("gx")) * LEAF, 8), LEAF)
    out[0:LEAF, :] = one_in[there, :] + two_in[there, :]
    direct = pl.ds(2 * LEAF, PAIR)
    out[LEAF:, :] = kept[LEAF : LEAF + PAIR, :] + (
        one_in[direct, :] + two_in[direct, :] + three_in[parity("gx")]
    )


def basis_kernel(pos, cell, count, after, basis, live, member, row):
    del after
    coords = [slots_down(pos[:, d, :]) for d in range(3)]
    for j, value in enumerate(harmonics(*coords)):
        basis[j] = value
    member[...] = member_t(cell, row).astype(BF16)
    live[...] = live_t(count, row).astype(F32)


def potential_kernel(
    kept, one_in, two_in, last, downward, basis, live, member, out, *scratch
):
    ops, spread, result, stage, done = scratch
    core = parity("gx")
    mine = pl.ds(pl.multiple_of(core * LEAF, 8), LEAF)
    leaf = kept[0:LEAF, :] + one_in[mine, :] + two_in[mine, :] + last[1 - core, 0:LEAF, :]
    coarse = last[0, LEAF:, :] + last[1, LEAF:, :]
    ops[...] = jnp.zeros_like(ops)
    octant = (parity("gx") * 2 + parity("gy")) * 2
    for c in range(2):
        ops[0:NP, c * PAD : c * PAD + NP] = octant_rows(downward, octant + c)
    even = even_lanes((PAD, NZ))
    columns = []
    for q in range(NQ):
        value = unpacked(coarse, q // 2, 2)
        if q % 2 == 0:
            down = [jnp.where(even, value, 0.0), jnp.where(even, 0.0, pltpu.roll(value, 1, 1))]
        else:
            down = [jnp.where(even, pltpu.roll(value, NZ - 1, 1), 0.0), jnp.where(even, 0.0, value)]
        columns.append(jnp.concatenate(down, axis=0))
    pushed = exact_dot(ops[0:PAD, :], jnp.concatenate(columns, axis=1))
    local = jnp.concatenate(
        [unpacked(leaf, q, NQ) + pushed[:, q * NZ : (q + 1) * NZ] for q in range(NQ)], axis=0
    )
    high, low = split(local)
    spread[...] = dot(high, member[...]) + dot(low, member[...])
    copies = [
        pltpu.make_async_copy(stage.at[0:SLOT], out.at[0:SLOT], done.at[0]),
        pltpu.make_async_copy(stage.at[SLOT:BLKS], out.at[SLOT:BLKS], done.at[1]),
    ]
    for start, size, lane in ((0, 64, 0), (64, 64, 0), (SLOT, EXTRA, SLOT)):
        totals = [None] * NQ
        for j in range(NP):
            value = basis[j, start : start + size, :]
            for q in range(NQ):
                term = spread[q * PAD + j : q * PAD + j + 1, lane : lane + SLOT]
                totals[q] = term if j == 0 else totals[q] + term * value
        for q in range(NQ):
            result[q, start : start + size, :] = jnp.where(
                live[start : start + size, :] > 0.0, totals[q], 0.0
            )
        if start == 64:
            for q in range(NQ):
                stage[0:SLOT, q, :] = result[q, 0:SLOT, :].T
            copies[0].start()
    for q in range(NQ):
        extra = result[q, SLOT:BLKS, :].T
        runs = [extra[g * EXTRA : (g + 1) * EXTRA, :] for g in range(4)]
        stage[SLOT:BLKS, q, :] = jnp.concatenate(runs, axis=1)
    copies[1].start()
    for copy in copies:
        copy.wait()


def call(kernel, outs, scratch, specs, name, micros=1, out_spec=VMEM):
    return pl.pallas_call(
        kernel,
        out_shape=outs if len(outs) > 1 else outs[0],
        in_specs=specs,
        out_specs=[out_spec] * len(outs) if len(outs) > 1 else out_spec,
        scratch_shapes=scratch,
        cost_estimate=pl.CostEstimate(
            flops=int(micros * 1e9), bytes_accessed=1000000, transcendentals=0
        ),
        compiler_params=pltpu.CompilerParams(vmem_limit_bytes=24 * 1024 * 1024),
        name=name,
    )


def rows(count):
    return jax.ShapeDtypeStruct((count, NZ), F32)


def chip_pairs():
    return [[i, i + 1] for i in range(0, lax.axis_size("gx"), 2)]


def outward_x(distance):
    peers = lax.axis_size("gx")
    return [(i, (i + distance if i % 2 else i - distance) % peers) for i in range(peers)]


def column_pairs(distance, above):
    wide, tall = lax.axis_size("gx"), lax.axis_size("gy")
    return [
        [(x + above) * tall + y, (x + 1 - above) * tall + (y + distance) % tall]
        for x in range(0, wide, 2)
        for y in range(tall)
    ]


def swap_y(field, distance):
    route = []
    for low, high in column_pairs(distance, 0):
        route += [(low, high), (high, low)]
    return lax.ppermute(field, ("gx", "gy"), route)


def translation_scratch(leaf_columns, coarse_columns):
    return [
        pltpu.VMEM((2, leaf_columns, LEAF, NZ), F32),
        pltpu.VMEM((2, coarse_columns, PAIR, NZ), F32),
        pltpu.VMEM((DEPTH, NQ * NZ), BF16),
        pltpu.VMEM((DEPTH, NQ * NZ), BF16),
        pltpu.VMEM((DEPTH, 2 * NZ), BF16),
        pltpu.VMEM((DEPTH, 2 * NZ), BF16),
    ]


def per_device(
    rel_pos,
    charges,
    block_cell,
    block_count,
    leaf_offsets,
    coarse_offsets,
    leaf_ops,
    coarse_ops,
    upward_ops,
    downward_ops,
):
    pos = rel_pos.reshape(3, BLKS, SLOT).transpose(1, 0, 2)
    charge = charges.reshape(NQ, BLKS, SLOT).transpose(1, 0, 2)
    cell = block_cell.reshape(1, BLKS)
    count = block_count.reshape(1, BLKS)
    upward = upward_ops.transpose(1, 0, 2)
    downward = downward_ops.transpose(1, 0, 2)
    index_row = pltpu.VMEM((1, LANES), jnp.int32)

    atoms = (pos, charge, cell, count, upward)
    own_field = call(
        moments_kernel,
        [rows(LEAF + PAIR)],
        [
            pltpu.VMEM((BLKS, 3, SLOT), F32),
            pltpu.VMEM((BLKS, NQ, SLOT), F32),
            pltpu.VMEM((1, BLKS), jnp.int32),
            pltpu.VMEM((1, BLKS), jnp.int32),
            pltpu.VMEM((NP, 8, NP), F32),
            pltpu.VMEM((NP, BLKS, SLOT), F32),
            pltpu.VMEM((NQ, BLKS, SLOT), F32),
            index_row,
            pltpu.VMEM((2 * PAD, PAD), F32),
            pltpu.SemaphoreType.DMA((5,)),
        ],
        [HBM] * 5,
        "moments",
        3,
    )(*[pltpu.with_memory_space_constraint(x, pltpu.HBM) for x in atoms])

    both = lax.all_gather(own_field, "gx", axis_index_groups=chip_pairs())
    near, parents = call(
        pair_kernel, [rows(2 * LEAF + PAIR), rows(PAIR)], [], [VMEM], "pair"
    )(both)
    beside = lax.ppermute(near, "gx", outward_x(1))
    beyond = lax.ppermute(parents, "gx", outward_x(3))
    leaf_table = jax.ShapeDtypeStruct((12 * PAD, DEPTH), BF16)
    coarse_table = jax.ShapeDtypeStruct((10 * PAD, DEPTH), BF16)
    leaf_near, leaf_far, coarse_near, coarse_far = call(
        tables_kernel,
        [leaf_table, leaf_table, coarse_table, coarse_table],
        [pltpu.VMEM((8, NZ), F32), pltpu.VMEM((TILES * PAD, 4 * NZ), F32)],
        [VMEM] * 4,
        "tables",
        2,
    )(
        leaf_offsets.T,
        coarse_offsets.T,
        leaf_ops.transpose(1, 2, 0),
        coarse_ops.transpose(1, 2, 0),
    )
    own_leaf, own_coarse = call(
        own_kernel,
        [
            jax.ShapeDtypeStruct((6 * PAD, NQ * NZ), F32),
            jax.ShapeDtypeStruct((5 * PAD, 2 * NZ), F32),
        ],
        translation_scratch(2, 1),
        [VMEM] * 3,
        "own",
        2,
    )(near, leaf_near, coarse_near)
    side = call(join_kernel, [rows(2 * LEAF + 2 * PAIR)], [], [VMEM] * 2, "join")(beside, beyond)
    sides = lax.all_gather(side, "gx", axis_index_groups=chip_pairs())

    one, two, kept = call(
        translate_kernel,
        [rows(2 * LEAF + 2 * PAIR), rows(2 * LEAF + 2 * PAIR), rows(LEAF + 2 * PAIR)],
        translation_scratch(4, 4),
        [VMEM] * 5,
        "translate",
        3,
    )(sides, leaf_far, coarse_far, own_leaf, own_coarse)

    one = swap_y(one, 1)
    two = swap_y(two, 2)
    relayed = call(relay_kernel, [rows(PAIR)], [], [VMEM] * 3, "relay")(kept, one, two)
    three = lax.all_gather(relayed, ("gx", "gy"), axis_index_groups=column_pairs(3, 1))
    basis, live, member = call(
        basis_kernel,
        [
            jax.ShapeDtypeStruct((NP, BLKS, SLOT), F32),
            jax.ShapeDtypeStruct((BLKS, SLOT), F32),
            jax.ShapeDtypeStruct((NZ, LANES), BF16),
        ],
        [index_row],
        [VMEM] * 4,
        "basis",
    )(pos, cell, count, kept)
    passed = call(exchange_kernel, [rows(LEAF + PAIR)], [], [VMEM] * 4, "exchange")(
        kept, one, two, three
    )
    last = lax.all_gather(passed, "gx", axis_index_groups=chip_pairs())

    potential = call(
        potential_kernel,
        [jax.ShapeDtypeStruct((BLKS, NQ, SLOT), F32)],
        [
            pltpu.VMEM((PAD, 2 * PAD), F32),
            pltpu.VMEM((NQ * PAD, LANES), F32),
            pltpu.VMEM((NQ, BLKS, SLOT), F32),
            pltpu.VMEM((BLKS, NQ, SLOT), F32),
            pltpu.SemaphoreType.DMA((2,)),
        ],
        [VMEM] * 8,
        "potential",
        3,
        HBM,
    )(kept, one, two, last, downward, basis, live, member)
    return potential.transpose(1, 0, 2).reshape(NQ, BLKS * SLOT)


def solution(mesh):
    in_specs = (
        P(None, ("gx", "gy")),
        P(None, ("gx", "gy")),
        P(("gx", "gy")),
        P(("gx", "gy")),
        P(),
        P(),
        P(),
        P(),
        P(),
        P(),
    )
    out_specs = P(None, ("gx", "gy"))
    return jax.shard_map(
        per_device, mesh=mesh, in_specs=in_specs, out_specs=out_specs, check_vma=False
    )
```

```python
import math

import jax
import jax.numpy as jnp
from jax import lax
from jax.experimental import pallas as pl
from jax.experimental.pallas import tpu as pltpu
from jax.sharding import PartitionSpec as P

NQ = 4
NP = 25
NZ = 128
BLKS = 160
LANES = 256
EXTRA = BLKS - 128
SLOT = 128
CLS = 96
PAD = 32
LEAF = 104
PAIR = 56
GROUP = 32
TILES = 7
DEPTH = TILES * NZ
F32 = jnp.float32
BF16 = jnp.bfloat16

VMEM = pl.BlockSpec(memory_space=pltpu.VMEM)
HBM = pl.BlockSpec(memory_space=pltpu.HBM)


def harmonics(pos_x, pos_y, pos_z):
    point_x = 2.0 * pos_x
    point_y = 2.0 * pos_y
    point_z = 2.0 * pos_z
    radius_sq = point_x * point_x + point_y * point_y + point_z * point_z
    real_part = {(0, 0): jnp.ones_like(point_x)}
    imag_part = {}
    for degree in range(1, 5):
        lower_real = real_part[degree - 1, degree - 1]
        if degree == 1:
            real_part[1, 1] = point_x * 0.5
            imag_part[1, 1] = point_y * 0.5
        else:
            lower_imag = imag_part[degree - 1, degree - 1]
            scale = 1.0 / (2.0 * degree)
            real_part[degree, degree] = (point_x * lower_real - point_y * lower_imag) * scale
            imag_part[degree, degree] = (point_x * lower_imag + point_y * lower_real) * scale
        for azimuth in range(degree):
            scale = 1.0 / float((degree + azimuth) * (degree - azimuth))
            scale_z = ((2.0 * degree - 1.0) * scale) * point_z
            if degree == 1:
                real_part[1, 0] = scale_z
                continue
            next_real = scale_z * real_part[degree - 1, azimuth]
            if degree - 2 >= azimuth:
                scaled_sq = radius_sq * scale
                next_real = next_real - scaled_sq * real_part[degree - 2, azimuth]
            real_part[degree, azimuth] = next_real
            if azimuth > 0:
                next_imag = scale_z * imag_part[degree - 1, azimuth]
                if degree - 2 >= azimuth:
                    next_imag = next_imag - scaled_sq * imag_part[degree - 2, azimuth]
                imag_part[degree, azimuth] = next_imag
    rows_out = []
    for degree in range(5):
        rows_out.append(real_part[degree, 0] * float(math.factorial(degree)))
        for azimuth in range(1, degree + 1):
            factor = math.sqrt(math.factorial(degree + azimuth) * math.factorial(degree - azimuth))
            rows_out.append(real_part[degree, azimuth] * factor)
            rows_out.append(imag_part[degree, azimuth] * factor)
    return rows_out


def split(value):
    high = value.astype(BF16)
    low = (value - high.astype(F32)).astype(BF16)
    return high, low


def dot(left, right):
    return lax.dot_general(left, right, (((1,), (0,)), ((), ())), preferred_element_type=F32)


def exact_dot(left, right):
    high, low = split(left)
    top, rest = split(right)
    both = dot(jnp.concatenate([high, low], axis=0), top)
    return both[: left.shape[0]] + both[left.shape[0] :] + dot(high, rest)


def unpacked(field, channel, channels):
    zeros = jnp.zeros((PAD - NP, NZ), F32)
    return jnp.concatenate(
        [
            field[channel * 24 : channel * 24 + 24],
            field[channels * 24 + channel : channels * 24 + channel + 1],
            zeros,
        ],
        axis=0,
    )


def store_packed(ref, base, channel, channels, value):
    ref[base + channel * 24 : base + channel * 24 + 24, :] = value[:24]
    row = base + channels * 24 + channel
    ref[row : row + 1, :] = value[24:25]


def even_lanes(shape):
    return lax.broadcasted_iota(jnp.int32, shape, 1) % 2 == 0


def octant_rows(ref, octant):
    return ref.reshape(NP * 8, NP)[pl.ds(octant, NP, stride=8), :]


def parity(axis):
    return lax.rem(lax.axis_index(axis), 2)


def slots_down(tile):
    extra = tile[SLOT:, :]
    runs = [extra[:, g * EXTRA : (g + 1) * EXTRA] for g in range(4)]
    return jnp.concatenate([tile[:SLOT, :].T, jnp.concatenate(runs, axis=0).T], axis=0)


def spread_row(values, row):
    row[:, 0:SLOT] = values[:, 0:SLOT]
    for g in range(4):
        row[:, SLOT + g * EXTRA : SLOT + (g + 1) * EXTRA] = values[:, SLOT:BLKS]
    return row[...]


def member_t(cell_ref, row):
    cells = lax.broadcasted_iota(jnp.int32, (NZ, LANES), 0)
    return (cells == spread_row(cell_ref, row)).astype(F32)


def live_t(count_ref, row):
    counts = spread_row(count_ref, row)
    first = lax.broadcasted_iota(jnp.int32, (SLOT, SLOT), 0)
    run = lax.broadcasted_iota(jnp.int32, (EXTRA, SLOT), 1) // EXTRA
    second = lax.broadcasted_iota(jnp.int32, (EXTRA, SLOT), 0) + run * EXTRA
    return jnp.concatenate([first < counts[:, :SLOT], second < counts[:, SLOT:]], axis=0)


def row_sums(parts):
    row = lax.broadcasted_iota(jnp.int32, parts[0].shape, 0)
    upper = row < 4
    parts = [
        jnp.where(upper, a, b) + pltpu.roll(jnp.where(upper, b, a), 4, 0)
        for a, b in zip(parts[:4], parts[4:])
    ]
    for distance in (2, 1):
        here = (row // distance) % 2 == 0
        half = len(parts) // 2
        parts = [
            jnp.where(here, a, b)
            + jnp.where(here, pltpu.roll(a, 8 - distance, 0), pltpu.roll(b, distance, 0))
            for a, b in zip(parts[:half], parts[half:])
        ]
    return parts[0]


def moments_kernel(
    pos_in, charge_in, cell_in, count_in, upward_in, out, *scratch
):
    pos, charge, cell, count, upward, basis, weight, row, ops, done = scratch
    copies = [
        pltpu.make_async_copy(source, target, done.at[n])
        for n, (source, target) in enumerate(
            (
                (pos_in, pos),
                (charge_in, charge),
                (cell_in, cell),
                (count_in, count),
                (upward_in, upward),
            )
        )
    ]
    for copy in copies:
        copy.start()
    copies[0].wait()
    coords = [slots_down(pos[:, d, :]) for d in range(3)]
    for j, value in enumerate(harmonics(*coords)):
        basis[j] = value
    for copy in copies[1:]:
        copy.wait()
    live = live_t(count, row)
    for q in range(NQ):
        weight[q] = jnp.where(live, slots_down(charge[:, q, :]), 0.0)

    def part(q, j):
        terms = weight[q] if j == 0 else weight[q] * basis[j]
        terms = terms.reshape(BLKS // 8, 8, SLOT)
        return jnp.concatenate(
            [jnp.sum(terms[: SLOT // 8], axis=0), jnp.sum(terms[SLOT // 8 :], axis=0)], axis=1
        )

    groups = [
        row_sums([part(q, j) for j in range(start, start + 8)])
        for q in range(NQ)
        for start in range(0, 24, 8)
    ]
    zeros = jnp.zeros((8, LANES), F32)
    groups.append(row_sums([part(q, 24) for q in range(NQ)] + [zeros] * 4))
    member = member_t(cell, row).T.astype(BF16)
    high, low = split(jnp.concatenate(groups, axis=0))
    field = dot(high, member) + dot(low, member)
    out[0:LEAF, :] = field
    ops[...] = jnp.zeros_like(ops)
    octant = (parity("gx") * 2 + parity("gy")) * 2
    for c in range(2):
        ops[c * PAD : c * PAD + NP, 0:NP] = octant_rows(upward, octant + c)
    stacked = jnp.concatenate([unpacked(field, q, NQ) for q in range(NQ)], axis=1)
    raised = exact_dot(ops[...], stacked)
    out[LEAF : LEAF + PAIR, :] = jnp.zeros((PAIR, NZ), F32)
    even = even_lanes((PAD, NZ))
    for pair in range(2):
        first, second = [
            [raised[c * PAD : (c + 1) * PAD, q * NZ : (q + 1) * NZ] for c in range(2)]
            for q in (2 * pair, 2 * pair + 1)
        ]
        value = jnp.where(
            even,
            first[0] + pltpu.roll(first[1], NZ - 1, 1),
            pltpu.roll(second[0], 1, 1) + second[1],
        )
        store_packed(out, LEAF, pair, 2, value)


def tables_kernel(leaf_at, coarse_at, leaf_ops, coarse_ops, *refs):
    codes, left = refs[4:]
    toward = (1 - 2 * parity("gx")).astype(F32)
    lane = lax.broadcasted_iota(jnp.int32, (NZ, NZ), 1).astype(F32)
    for at, ops, outs, columns, reaches in (
        (leaf_at, leaf_ops, refs[0:2], 2, (0, 1, 2)),
        (coarse_at, coarse_ops, refs[2:4], 1, (0, 1, 2, -1, -2)),
    ):
        codes[...] = jnp.full((8, NZ), 99.0, F32)
        codes[0:3, 0:CLS] = at[...].astype(F32)
        turned = codes[...].T
        ahead = [-toward * turned[:, 1:2] == float(r) for r in reaches]
        places = []
        for own in (True, False):
            for t in range(columns):
                source = turned[:, 0:1] + float(2 + t)
                near = (source >= 2.0) & (source < float(2 + columns))
                if own:
                    chosen, column = near, source - 2.0
                else:
                    chosen = jnp.logical_not(near)
                    column = jnp.where(source < 2.0, source, source - float(columns))
                place = column * 8.0 + 3.0 - turned[:, 2:3]
                places.append(jnp.where(chosen, place, -1000.0))
        picks = []
        for part in range(4):
            blocks = []
            for place in places:
                found = lane == place + float(part * GROUP)
                blocks += [(found & row).astype(BF16) for row in ahead]
            picks.append(jnp.concatenate(blocks, axis=1))
        pick = jnp.concatenate(picks, axis=0)
        left[...] = jnp.zeros_like(left)
        for i in range(NP):
            row = (i // 4) * PAD
            col = (i % 4) * NZ
            left[row : row + NP, col : col + CLS] = ops[:, i, :]
        blocks = columns * len(reaches)
        for part, value in enumerate(split(left[...])):
            table = dot(value, pick).astype(BF16)
            for side, out in enumerate(outs):
                for tile in range(TILES):
                    for block in range(blocks):
                        row = (part * blocks + block) * PAD
                        col = (side * blocks + block) * NZ
                        out[row : row + PAD, tile * NZ : (tile + 1) * NZ] = table[
                            tile * PAD : (tile + 1) * PAD, col : col + NZ
                        ]


def pair_kernel(near, fields, parents):
    fields[0:LEAF, :] = near[0, 0:LEAF, :]
    fields[LEAF : 2 * LEAF, :] = near[1, 0:LEAF, :]
    total = near[0, LEAF:, :] + near[1, LEAF:, :]
    fields[2 * LEAF :, :] = total
    parents[...] = total


def join_kernel(fields, far, out):
    out[0 : 2 * LEAF + PAIR, :] = fields[...]
    out[2 * LEAF + PAIR :, :] = far[...]


def back(target, column, value, step):
    value = pltpu.roll(value, NZ - 3 * step, 1)
    top = value.astype(BF16).astype(F32)
    target[0, column] = top
    target[1, column] = value - top


def spread(source, columns, high, low, step):
    channels = high.shape[1] // NZ
    used = NP * GROUP
    for ref in (high, low):
        ref[used:, :] = jnp.zeros((DEPTH - used, ref.shape[1]), BF16)

    def turned(part, column, at):
        if column is None:
            return jnp.zeros((8, NZ), F32)
        value = jnp.broadcast_to(source[part, column, at : at + 1, :], (8, NZ))
        return pltpu.roll(value, 0, 1, stride=step, stride_axis=0)

    for i in range(NP):
        for two in range(2):
            base = i * GROUP + two * 16
            members = columns[2 * two : 2 * two + 2]
            for part, ref in enumerate((high, low)):
                if not members:
                    ref[base : base + 16, :] = jnp.zeros((16, ref.shape[1]), BF16)
                    continue
                for q in range(channels):
                    at = q * 24 + i if i < 24 else channels * 24 + q
                    value = jnp.concatenate(
                        [turned(part, column, at) for column in members], axis=0
                    )
                    ref[base : base + 16, q * NZ : (q + 1) * NZ] = value.astype(BF16)


def product(table, high, low):
    height = table.shape[0] // 2
    both = dot(table[...], high[...])
    return both[:height] + both[height:] + dot(table[0:height, :], low[...])


def own_kernel(near, leaf_k, coarse_k, leaf_out, coarse_out, *scratch):
    fields, parents, high, low, coarse_high, coarse_low = scratch
    back(parents, 0, near[2 * LEAF :, :], 2)
    for a in range(2):
        back(fields, a, near[a * LEAF : (a + 1) * LEAF, :], 1)
    spread(parents, [0, None], coarse_high, coarse_low, 2)
    spread(fields, [0, 1], high, low, 1)
    coarse_out[...] = product(coarse_k, coarse_high, coarse_low)
    leaf_out[...] = product(leaf_k, high, low)


def translate_kernel(sides, leaf_k, coarse_k, own_leaf, own_coarse, *refs):
    one_out, two_out, kept, fields, parents, high, low, coarse_high, coarse_low = refs
    core = parity("gx")

    def emit(ref, base, value, channels, rows):
        ref[base + channels * 25 : base + rows, :] = jnp.zeros((rows - channels * 25, NZ), F32)
        for q in range(channels):
            store_packed(ref, base, q, channels, value[:, q * NZ : (q + 1) * NZ])

    one, two = 2 * LEAF, 2 * LEAF + PAIR
    back(parents, 0, sides[0, two:, :], 2)
    back(parents, 1, sides[0, one:two, :], 2)
    back(parents, 2, sides[1, one:two, :], 2)
    back(parents, 3, sides[1, two:, :], 2)
    for a in range(2):
        back(fields, a, sides[0, a * LEAF : (a + 1) * LEAF, :], 1)
        back(fields, 2 + a, sides[1, a * LEAF : (a + 1) * LEAF, :], 1)
    spread(fields, [0, 1, 2, 3], high, low, 1)
    result = product(leaf_k, high, low) + own_leaf[...]
    blocks = [result[b * PAD : (b + 1) * PAD] for b in range(6)]
    spread(parents, [0, 1, 2, 3], coarse_high, coarse_low, 2)
    result = product(coarse_k, coarse_high, coarse_low) + own_coarse[...]
    coarse = [result[b * PAD : (b + 1) * PAD] for b in range(5)]
    for t in range(2):
        emit(one_out, t * LEAF, blocks[3 * t + 1], NQ, LEAF)
        emit(two_out, t * LEAF, blocks[3 * t + 2], NQ, LEAF)
    emit(kept, 0, jnp.where(core == 0, blocks[0], blocks[3]), NQ, LEAF)
    blocks = coarse
    outer = lax.rem(core + parity("gy"), 2) == 1
    emit(kept, LEAF, jnp.where(core == 0, blocks[0], 0.0), 2, PAIR)
    emit(kept, LEAF + PAIR, jnp.where(outer, blocks[3], blocks[4]), 2, PAIR)
    emit(one_out, 2 * LEAF, jnp.where(outer, blocks[1], blocks[0]), 2, PAIR)
    emit(one_out, 2 * LEAF + PAIR, blocks[2], 2, PAIR)
    emit(two_out, 2 * LEAF, blocks[1], 2, PAIR)
    emit(two_out, 2 * LEAF + PAIR, jnp.where(outer, 0.0, blocks[2]), 2, PAIR)


def relay_kernel(kept, one_in, two_in, out):
    relayed = one_in[2 * LEAF + PAIR :, :] + two_in[2 * LEAF + PAIR :, :]
    out[...] = kept[LEAF + PAIR :, :] + relayed


def exchange_kernel(kept, one_in, two_in, three_in, out):
    there = pl.ds(pl.multiple_of((1 - parity("gx")) * LEAF, 8), LEAF)
    out[0:LEAF, :] = one_in[there, :] + two_in[there, :]
    direct = pl.ds(2 * LEAF, PAIR)
    out[LEAF:, :] = kept[LEAF : LEAF + PAIR, :] + (
        one_in[direct, :] + two_in[direct, :] + three_in[parity("gx")]
    )


def basis_kernel(pos, cell, count, after, basis, live, member, row):
    del after
    coords = [slots_down(pos[:, d, :]) for d in range(3)]
    for j, value in enumerate(harmonics(*coords)):
        basis[j] = value
    member[...] = member_t(cell, row).astype(BF16)
    live[...] = live_t(count, row).astype(F32)


def potential_kernel(
    kept, one_in, two_in, last, downward, basis, live, member, out, *scratch
):
    ops, spread, result, stage, done = scratch
    core = parity("gx")
    mine = pl.ds(pl.multiple_of(core * LEAF, 8), LEAF)
    leaf = kept[0:LEAF, :] + one_in[mine, :] + two_in[mine, :] + last[1 - core, 0:LEAF, :]
    coarse = last[0, LEAF:, :] + last[1, LEAF:, :]
    ops[...] = jnp.zeros_like(ops)
    octant = (parity("gx") * 2 + parity("gy")) * 2
    for c in range(2):
        ops[0:NP, c * PAD : c * PAD + NP] = octant_rows(downward, octant + c)
    even = even_lanes((PAD, NZ))
    columns = []
    for q in range(NQ):
        value = unpacked(coarse, q // 2, 2)
        if q % 2 == 0:
            down = [jnp.where(even, value, 0.0), jnp.where(even, 0.0, pltpu.roll(value, 1, 1))]
        else:
            down = [jnp.where(even, pltpu.roll(value, NZ - 1, 1), 0.0), jnp.where(even, 0.0, value)]
        columns.append(jnp.concatenate(down, axis=0))
    pushed = exact_dot(ops[0:PAD, :], jnp.concatenate(columns, axis=1))
    local = jnp.concatenate(
        [unpacked(leaf, q, NQ) + pushed[:, q * NZ : (q + 1) * NZ] for q in range(NQ)], axis=0
    )
    high, low = split(local)
    spread[...] = dot(high, member[...]) + dot(low, member[...])
    copies = [
        pltpu.make_async_copy(stage.at[0:SLOT], out.at[0:SLOT], done.at[0]),
        pltpu.make_async_copy(stage.at[SLOT:BLKS], out.at[SLOT:BLKS], done.at[1]),
    ]
    for start, size, lane in ((0, 64, 0), (64, 64, 0), (SLOT, EXTRA, SLOT)):
        totals = [None] * NQ
        for j in range(NP):
            value = basis[j, start : start + size, :]
            for q in range(NQ):
                term = spread[q * PAD + j : q * PAD + j + 1, lane : lane + SLOT]
                totals[q] = term if j == 0 else totals[q] + term * value
        for q in range(NQ):
            result[q, start : start + size, :] = jnp.where(
                live[start : start + size, :] > 0.0, totals[q], 0.0
            )
        if start == 64:
            for q in range(NQ):
                stage[0:SLOT, q, :] = result[q, 0:SLOT, :].T
            copies[0].start()
    for q in range(NQ):
        extra = result[q, SLOT:BLKS, :].T
        runs = [extra[g * EXTRA : (g + 1) * EXTRA, :] for g in range(4)]
        stage[SLOT:BLKS, q, :] = jnp.concatenate(runs, axis=1)
    copies[1].start()
    for copy in copies:
        copy.wait()


def call(kernel, outs, scratch, specs, name, micros=1, out_spec=VMEM):
    return pl.pallas_call(
        kernel,
        out_shape=outs if len(outs) > 1 else outs[0],
        in_specs=specs,
        out_specs=[out_spec] * len(outs) if len(outs) > 1 else out_spec,
        scratch_shapes=scratch,
        cost_estimate=pl.CostEstimate(
            flops=int(micros * 1e9), bytes_accessed=1000000, transcendentals=0
        ),
        compiler_params=pltpu.CompilerParams(vmem_limit_bytes=24 * 1024 * 1024),
        name=name,
    )


def rows(count):
    return jax.ShapeDtypeStruct((count, NZ), F32)


def chip_pairs():
    return [[i, i + 1] for i in range(0, lax.axis_size("gx"), 2)]


def outward_x(distance):
    peers = lax.axis_size("gx")
    return [(i, (i + distance if i % 2 else i - distance) % peers) for i in range(peers)]


def column_pairs(distance, above):
    wide, tall = lax.axis_size("gx"), lax.axis_size("gy")
    return [
        [(x + above) * tall + y, (x + 1 - above) * tall + (y + distance) % tall]
        for x in range(0, wide, 2)
        for y in range(tall)
    ]


def swap_y(field, distance):
    route = []
    for low, high in column_pairs(distance, 0):
        route += [(low, high), (high, low)]
    return lax.ppermute(field, ("gx", "gy"), route)


def translation_scratch(leaf_columns, coarse_columns):
    return [
        pltpu.VMEM((2, leaf_columns, LEAF, NZ), F32),
        pltpu.VMEM((2, coarse_columns, PAIR, NZ), F32),
        pltpu.VMEM((DEPTH, NQ * NZ), BF16),
        pltpu.VMEM((DEPTH, NQ * NZ), BF16),
        pltpu.VMEM((DEPTH, 2 * NZ), BF16),
        pltpu.VMEM((DEPTH, 2 * NZ), BF16),
    ]


def per_device(
    rel_pos,
    charges,
    block_cell,
    block_count,
    leaf_offsets,
    coarse_offsets,
    leaf_ops,
    coarse_ops,
    upward_ops,
    downward_ops,
):
    pos = rel_pos.reshape(3, BLKS, SLOT).transpose(1, 0, 2)
    charge = charges.reshape(NQ, BLKS, SLOT).transpose(1, 0, 2)
    cell = block_cell.reshape(1, BLKS)
    count = block_count.reshape(1, BLKS)
    upward = upward_ops.transpose(1, 0, 2)
    downward = downward_ops.transpose(1, 0, 2)
    index_row = pltpu.VMEM((1, LANES), jnp.int32)

    atoms = (pos, charge, cell, count, upward)
    own_field = call(
        moments_kernel,
        [rows(LEAF + PAIR)],
        [
            pltpu.VMEM((BLKS, 3, SLOT), F32),
            pltpu.VMEM((BLKS, NQ, SLOT), F32),
            pltpu.VMEM((1, BLKS), jnp.int32),
            pltpu.VMEM((1, BLKS), jnp.int32),
            pltpu.VMEM((NP, 8, NP), F32),
            pltpu.VMEM((NP, BLKS, SLOT), F32),
            pltpu.VMEM((NQ, BLKS, SLOT), F32),
            index_row,
            pltpu.VMEM((2 * PAD, PAD), F32),
            pltpu.SemaphoreType.DMA((5,)),
        ],
        [HBM] * 5,
        "moments",
        3,
    )(*[pltpu.with_memory_space_constraint(x, pltpu.HBM) for x in atoms])

    both = lax.all_gather(own_field, "gx", axis_index_groups=chip_pairs())
    near, parents = call(
        pair_kernel, [rows(2 * LEAF + PAIR), rows(PAIR)], [], [VMEM], "pair"
    )(both)
    beside = lax.ppermute(near, "gx", outward_x(1))
    beyond = lax.ppermute(parents, "gx", outward_x(3))
    leaf_table = jax.ShapeDtypeStruct((12 * PAD, DEPTH), BF16)
    coarse_table = jax.ShapeDtypeStruct((10 * PAD, DEPTH), BF16)
    leaf_near, leaf_far, coarse_near, coarse_far = call(
        tables_kernel,
        [leaf_table, leaf_table, coarse_table, coarse_table],
        [pltpu.VMEM((8, NZ), F32), pltpu.VMEM((TILES * PAD, 4 * NZ), F32)],
        [VMEM] * 4,
        "tables",
        2,
    )(
        leaf_offsets.T,
        coarse_offsets.T,
        leaf_ops.transpose(1, 2, 0),
        coarse_ops.transpose(1, 2, 0),
    )
    own_leaf, own_coarse = call(
        own_kernel,
        [
            jax.ShapeDtypeStruct((6 * PAD, NQ * NZ), F32),
            jax.ShapeDtypeStruct((5 * PAD, 2 * NZ), F32),
        ],
        translation_scratch(2, 1),
        [VMEM] * 3,
        "own",
        2,
    )(near, leaf_near, coarse_near)
    side = call(join_kernel, [rows(2 * LEAF + 2 * PAIR)], [], [VMEM] * 2, "join")(beside, beyond)
    sides = lax.all_gather(side, "gx", axis_index_groups=chip_pairs())

    one, two, kept = call(
        translate_kernel,
        [rows(2 * LEAF + 2 * PAIR), rows(2 * LEAF + 2 * PAIR), rows(LEAF + 2 * PAIR)],
        translation_scratch(4, 4),
        [VMEM] * 5,
        "translate",
        3,
    )(sides, leaf_far, coarse_far, own_leaf, own_coarse)

    one = swap_y(one, 1)
    two = swap_y(two, 2)
    relayed = call(relay_kernel, [rows(PAIR)], [], [VMEM] * 3, "relay")(kept, one, two)
    three = lax.all_gather(relayed, ("gx", "gy"), axis_index_groups=column_pairs(3, 1))
    basis, live, member = call(
        basis_kernel,
        [
            jax.ShapeDtypeStruct((NP, BLKS, SLOT), F32),
            jax.ShapeDtypeStruct((BLKS, SLOT), F32),
            jax.ShapeDtypeStruct((NZ, LANES), BF16),
        ],
        [index_row],
        [VMEM] * 4,
        "basis",
    )(pos, cell, count, kept)
    passed = call(exchange_kernel, [rows(LEAF + PAIR)], [], [VMEM] * 4, "exchange")(
        kept, one, two, three
    )
    last = lax.all_gather(passed, "gx", axis_index_groups=chip_pairs())

    potential = call(
        potential_kernel,
        [jax.ShapeDtypeStruct((BLKS, NQ, SLOT), F32)],
        [
            pltpu.VMEM((PAD, 2 * PAD), F32),
            pltpu.VMEM((NQ * PAD, LANES), F32),
            pltpu.VMEM((NQ, BLKS, SLOT), F32),
            pltpu.VMEM((BLKS, NQ, SLOT), F32),
            pltpu.SemaphoreType.DMA((2,)),
        ],
        [VMEM] * 8,
        "potential",
        3,
        HBM,
    )(kept, one, two, last, downward, basis, live, member)
    return potential.transpose(1, 0, 2).reshape(NQ, BLKS * SLOT)


def solution(mesh):
    in_specs = (
        P(None, ("gx", "gy")),
        P(None, ("gx", "gy")),
        P(("gx", "gy")),
        P(("gx", "gy")),
        P(),
        P(),
        P(),
        P(),
        P(),
        P(),
    )
    out_specs = P(None, ("gx", "gy"))
    return jax.shard_map(
        per_device, mesh=mesh, in_specs=in_specs, out_specs=out_specs, check_vma=False
    )
```
